256 devices in a mesh: src: 64 (over z, x, core), tgt: 4 (over y).
Axes of the slice: x: 4, y: 4, z: 8, core: 2. Of those that a mesh axis runs over, the one named last changes fastest.
Arguments:
- source_points: float32 [64, 65536], P(None, 'src'), may hold values from -24 to 24
- target_points: float32 [64, 16384], P(None, 'tgt'), may hold values from -24 to 24
- log_source_mass: float32 [65536], P('src'), may hold values from -1 to 1
- log_target_mass: float32 [16384], P('tgt'), may hold values from -1 to 1
Outputs:
- source_potential: float32 [65536], P('src')
- target_potential: float32 [16384], P('tgt')
- source_gradient: float32 [64, 65536], P(None, 'src')
- target_gradient: float32 [64, 4, 4096], P(None, 'tgt', 'src')
The draws below stay inside these ranges and needn't reach their ends.
All inputs are finite; a program needn't handle non-finite values.
Results may differ from the reference program's by a relative error of at most 0.0003.
Values sent between devices are 32-bit elements; how exact they have to be, the bound alone decides.
A program may use at most 128 MiB of HBM per device.

```python
import jax
import jax.numpy as jnp
from jax import lax

E = 64
S_DEV = 1024
T_DEV = 4096
ITERS = 2
NS = 65536
NT = 16384
N_TGT = 4


def shared_targets(key):
    return jnp.clip(jax.random.normal(key, (E, NT), jnp.float32), -6.0, 6.0)


def draw_target_points(key, part):
    base = shared_targets(key)
    return base


def draw_source_points(key, part):
    key = jax.random.fold_in(key, 7)
    own = jnp.clip(jax.random.normal(key, (E, NS), jnp.float32), -6.0, 6.0)
    return own


def levels(key, dims, shards, smallest, top_value):
    level = 1.0
    for dim, parts in shards:
        steps = jax.random.uniform(jax.random.fold_in(jax.random.fold_in(key, 6), dim), (parts,), jnp.float32, smallest / len(shards), top_value / len(shards))
        level = level * jnp.repeat(jnp.exp(steps), dims[dim] // parts).reshape((-1,) + (1,) * (len(dims) - 1 - dim))
    return level


def setup_inputs(seed: int = 0) -> dict:
    key_list = jax.random.split(jax.random.key(seed), 5)
    source_points = draw_source_points(jax.random.fold_in(key_list[4], 71), 0)
    target_points = draw_target_points(jax.random.fold_in(key_list[4], 71), 0)
    log_source_mass = jnp.clip(jax.random.uniform(key_list[2], (NS,), jnp.float32, -1.0, 1.0) * levels(key_list[2], (NS,), ((0, 64),), -0.4, 0.0), -1.0, 1.0)
    log_target_mass = jnp.clip(jax.random.uniform(key_list[3], (NT,), jnp.float32, -1.0, 1.0) * levels(key_list[3], (NT,), ((0, 4),), -0.4, 0.0), -1.0, 1.0)
    return {"source_points": source_points, "target_points": target_points, "log_source_mass": log_source_mass, "log_target_mass": log_target_mass}


EPSILON = 0.05


def pair_cost(points_a, points_b):
    cross = lax.dot_general(points_a, points_b, (((0,), (0,)), ((), ())), precision=lax.Precision.HIGHEST, preferred_element_type=jnp.float32)
    norms_a = jnp.sum(points_a * points_a, 0)
    norms_b = jnp.sum(points_b * points_b, 0)
    return (norms_a[:, None] + norms_b[None, :] - 2.0 * cross) / E


def reference(source_points, target_points, log_source_mass, log_target_mass):
    blocks = NS // S_DEV
    src_blocks = source_points.reshape(E, blocks, S_DEV).transpose(1, 0, 2)
    mass_blocks = log_source_mass.reshape(blocks, S_DEV)

    def update_source(target_pot):
        def one_block(points):
            cost = pair_cost(points, target_points)
            scores = log_target_mass[None, :] + (target_pot[None, :] - cost) / EPSILON
            top = jnp.max(scores, 1)
            return -EPSILON * (top + jnp.log(jnp.sum(jnp.exp(scores - top[:, None]), 1)))
        return lax.map(one_block, src_blocks).reshape(NS)

    def update_target(source_pot):
        pot_blocks = source_pot.reshape(blocks, S_DEV)

        def one_block(item):
            points, masses, potent = item
            cost = pair_cost(points, target_points)
            scores = masses[:, None] + (potent[:, None] - cost) / EPSILON
            top = jnp.max(scores, 0)
            return top, jnp.sum(jnp.exp(scores - top[None, :]), 0)
        tops, totals = lax.map(one_block, (src_blocks, mass_blocks, pot_blocks))
        top = jnp.max(tops, 0)
        total = jnp.sum(totals * jnp.exp(tops - top[None, :]), 0)
        return -EPSILON * (top + jnp.log(total))

    target_pot = jnp.zeros((NT,), jnp.float32)
    source_pot = jnp.zeros((NS,), jnp.float32)
    for step in range(ITERS):
        source_pot = update_source(target_pot)
        target_pot = update_target(source_pot)
    pot_blocks = source_pot.reshape(blocks, S_DEV)

    def plan_block(carry, item):
        points, masses, potent = item
        cost = pair_cost(points, target_points)
        plan = jnp.exp(masses[:, None] + log_target_mass[None, :] + (potent[:, None] + target_pot[None, :] - cost) / EPSILON)
        moved = lax.dot_general(target_points, plan, (((1,), (1,)), ((), ())), precision=lax.Precision.HIGHEST, preferred_element_type=jnp.float32)
        grad_block = points * jnp.sum(plan, 1)[None, :] - moved
        pulled = lax.dot_general(points, plan, (((1,), (0,)), ((), ())), precision=lax.Precision.HIGHEST, preferred_element_type=jnp.float32)
        carry = carry + target_points * jnp.sum(plan, 0)[None, :] - pulled
        return carry, grad_block

    start = jnp.zeros((E, NT), jnp.float32)
    target_grad, grad_blocks = lax.scan(plan_block, start, (src_blocks, mass_blocks, pot_blocks))
    source_grad = grad_blocks.transpose(1, 0, 2).reshape(E, NS)
    return source_pot, target_pot, source_grad, target_grad.reshape(E, N_TGT, T_DEV)
```

```python
import functools

import jax
import jax.numpy as jnp
import numpy as np
from jax import lax
from jax.experimental import pallas as pl
from jax.experimental.pallas import tpu as pltpu
from jax.sharding import PartitionSpec as P

EPSILON = 0.05
LOG2E = float(np.log2(np.e))
BETA = LOG2E / EPSILON
MESH = pl.DeviceIdType.MESH
F32 = jnp.float32
BF16 = jnp.bfloat16


def split3(a):
    hi = a.astype(BF16)
    rest = a - hi.astype(F32)
    mid = rest.astype(BF16)
    lo = (rest - mid.astype(F32)).astype(BF16)
    return hi, mid, lo


class Exchange:
    def __init__(self, sems, me, n, device):
        self.send, self.recv, self.base = sems
        self.me, self.n, self.device = me, n, device

    def copy(self, r, src, dst):
        peer = lax.rem(self.me + r, self.n)
        return pltpu.make_async_remote_copy(
            src_ref=src(peer),
            dst_ref=dst(self.me),
            send_sem=self.send.at[self.base + r - 1],
            recv_sem=self.recv.at[self.base + r - 1],
            device_id=self.device(peer),
            device_id_type=MESH,
        )

    def start(self, src, dst):
        self.copies = [self.copy(r, src, dst) for r in range(1, self.n)]
        for copy in self.copies:
            copy.start()

    def wait_recv(self):
        for copy in self.copies:
            copy.wait_recv()

    def wait_send(self):
        for copy in self.copies:
            copy.wait_send()


def kernel(dims, x_ref, y_ref, la_ref, lb_ref,
           f_out, g_out, sg_out, tg_out,
           p_ref, hi_ref, lo_ref, xk_ref, yk_ref, mx_ref, sm_ref, vb_ref,
           fm_ref, fr_ref, mg_ref, ga_ref, gb_ref, gf_ref, w_ref, k_ref,
           ca_ref, cs_ref, cb_ref, d_ref, a_ref, xa_ref, yb_ref,
           u_ref, r0_ref, t1_ref, r1_ref, t2_ref, r2_ref, r3_ref,
           so_ref, sr_ref, sgb_ref, send_sems, recv_sems):
    NX, NZ, NY = dims
    NQ = 2 * NX
    E, S = x_ref.shape
    T = y_ref.shape[1]
    CB = T // NZ
    RB = S // NY
    TB = CB // 128
    NT = T // 128
    RS = 128

    src = lax.axis_index("src")
    me_y = lax.axis_index("tgt")
    me_z = src // NQ
    me_q = lax.rem(src, NQ)
    me_x = me_q // 2
    me_c = lax.rem(me_q, 2)

    dev_y = lambda j: {"tgt": j}
    dev_z = lambda j: {"src": j * NQ + me_q}
    dev_q = lambda j: {"src": me_z * NQ + j}
    dev_x = lambda j: {"src": me_z * NQ + j * 2 + me_c}
    dev_c = lambda j: {"src": me_z * NQ + me_x * 2 + j}

    taken = [0]

    def group(me, n, device):
        base = taken[0]
        taken[0] += n - 1
        return Exchange((send_sems, recv_sems, base), me, n, device)

    barrier = pltpu.get_barrier_semaphore()
    partners = 0
    for me, n, device in ((me_y, NY, dev_y), (me_z, NZ, dev_z), (me_q, NQ, dev_q)):
        for r in range(1, n):
            pl.semaphore_signal(barrier, inc=1, device_id=device(lax.rem(me + r, n)), device_id_type=MESH)
            partners += 1

    def prep_y(b, _):
        cols = pl.ds(pl.multiple_of(b * CB, CB), CB)
        y = y_ref[:, cols]
        y1, y2, y3 = split3(y)
        for n, part in enumerate((y1, y2, y1, y3, y2, y1)):
            yk_ref[n * E:(n + 1) * E, cols] = part
        u = LOG2E * lb_ref[:, cols] - (BETA / E) * jnp.sum(y * y, 0, keepdims=True)
        u1, u2, u3 = split3(u)
        row = lax.broadcasted_iota(jnp.int32, (16, CB), 0)
        pick = lambda n, v: jnp.where(row == n, jnp.broadcast_to(v.astype(F32), (16, CB)), 0.0)
        yk_ref[6 * E:6 * E + 16, cols] = (pick(0, u1) + pick(1, u2) + pick(2, u3)).astype(BF16)
        yk_ref[6 * E + 16:8 * E, cols] = jnp.zeros((2 * E - 16, CB), BF16)
        return 0

    lax.fori_loop(0, NZ, prep_y, 0)

    lane = lax.broadcasted_iota(jnp.int32, (128, 128), 1)
    left = lane < E

    def prep_x(i, _):
        rows = pl.ds(pl.multiple_of(i * 128, 128), 128)
        x = x_ref[:, rows] * (2.0 * BETA / E)
        x1, x2, x3 = (v.astype(F32) for v in split3(jnp.concatenate([x, x], 0).T))
        xk_ref[rows, 0:128] = x1.astype(BF16)
        xk_ref[rows, 128:256] = jnp.where(left, x2, x1).astype(BF16)
        xk_ref[rows, 256:384] = jnp.where(left, x2, x3).astype(BF16)
        xk_ref[rows, 384:512] = jnp.where(lane < 3, 1.0, 0.0).astype(BF16)
        mx_ref[rows, :] = jnp.full((128, 128), -3e38, F32)
        return 0

    lax.fori_loop(0, S // 128, prep_x, 0)

    def scores(b, _):
        cols = pl.ds(pl.multiple_of(b * CB, CB), CB)
        yk = yk_ref[:, cols]
        for i in range(S // RS):
            rows = slice(i * RS, (i + 1) * RS)
            s = jnp.dot(xk_ref[rows, :], yk, preferred_element_type=F32)
            p_ref[rows, cols] = s
            m = mx_ref[rows, :]
            for t in range(TB):
                m = jnp.maximum(m, s[:, t * 128:(t + 1) * 128])
            mx_ref[rows, :] = m
        return 0

    lax.fori_loop(0, NZ, scores, 0)

    def row_sums(i, _):
        rows = pl.ds(pl.multiple_of(i * 16, 16), 16)
        m = mx_ref[rows, :]
        acc = [jnp.zeros((16, 128), F32) for _ in range(2)]
        for t in range(NT):
            acc[t % 2] += jnp.exp2(p_ref[rows, t * 128:(t + 1) * 128] - m)
        sm_ref[rows, :] = acc[0] + acc[1]
        return 0

    lax.fori_loop(0, S // 16, row_sums, 0)

    for i in range(S // 128):
        rows = slice(i * 128, (i + 1) * 128)
        m = mx_ref[rows, :].T
        top = jnp.max(m, 0, keepdims=True)
        total = jnp.sum(sm_ref[rows, :].T * jnp.exp2(m - top), 0, keepdims=True)
        fm_ref[me_y, 0:1, rows] = top
        fm_ref[me_y, 1:2, rows] = total

    pl.semaphore_wait(barrier, partners)
    f1 = group(me_y, NY, dev_y)
    f1.start(lambda peer: fm_ref.at[me_y], lambda me: fm_ref.at[me])
    f1.wait_recv()

    def combine(ref, n):
        top = ref[0, 0:1, :]
        for j in range(1, n):
            top = jnp.maximum(top, ref[j, 0:1, :])
        total = ref[0, 1:2, :] * jnp.exp2(ref[0, 0:1, :] - top)
        for j in range(1, n):
            total = total + ref[j, 1:2, :] * jnp.exp2(ref[j, 0:1, :] - top)
        return top, total

    def add_up(ref, n):
        total = ref[0]
        for j in range(1, n):
            total = total + ref[j]
        return total

    def spread(row):
        for i in range(S // 128):
            part = row[:, i * 128:(i + 1) * 128]
            vb_ref[i * 128:(i + 1) * 128, :] = jnp.broadcast_to(part, (128, 128)).T

    top, total = combine(fm_ref, NY)
    lse = top + jnp.log2(total)
    la2 = LOG2E * la_ref[...]
    spread(la2 - lse)

    def columns(b, _):
        cols = pl.ds(pl.multiple_of(b * CB, CB), CB)

        def scored(i):
            rows = pl.ds(pl.multiple_of(i * RS, RS), RS)
            v = vb_ref[rows, :]
            return p_ref[rows, cols] + jnp.concatenate([v] * TB, 1)

        def find(i, m):
            return jnp.maximum(m, jnp.max(scored(i).reshape(RS // 8, 8, CB), 0))

        m = lax.fori_loop(0, S // RS, find, jnp.full((8, CB), -3e38, F32))
        m = jnp.max(m, 0, keepdims=True)

        def weigh(i, acc):
            rows = pl.ds(pl.multiple_of(i * RS, RS), RS)
            e = jnp.exp2(scored(i) - m)
            p_ref[rows, cols] = e
            return acc + jnp.sum(e.reshape(RS // 8, 8, CB), 0)

        acc = lax.fori_loop(0, S // RS, weigh, jnp.zeros((8, CB), F32))
        mg_ref[b, 0:1, :] = m
        mg_ref[b, 1:2, :] = jnp.sum(acc, 0, keepdims=True)
        return 0

    lax.fori_loop(0, NZ, columns, 0)

    gA = group(me_q, NQ, dev_q)
    gA.start(lambda peer: mg_ref.at[peer], lambda me: ga_ref.at[me])
    ga_ref[me_q] = mg_ref[me_q]

    def split_rows(first, last):
        def body(i, _):
            rows = pl.ds(pl.multiple_of(i * 16, 16), 16)
            for t in range(NT // 4):
                lanes = slice(t * 512, (t + 1) * 512)
                e = p_ref[rows, lanes]
                hi = e.astype(BF16)
                hi_ref[rows, lanes] = hi
                lo_ref[rows, lanes] = (e - hi.astype(F32)).astype(BF16)
            return 0

        lax.fori_loop(first, last, body, 0)

    strips = S // 16
    split_rows(0, strips // 3)
    gA.wait_recv()
    top, total = combine(ga_ref, NQ)
    gb_ref[me_z, 0:1, :] = top
    gb_ref[me_z, 1:2, :] = total
    gB = group(me_z, NZ, dev_z)
    gB.start(lambda peer: gb_ref.at[me_z], lambda me: gb_ref.at[me])
    split_rows(strips // 3, 2 * strips // 3)
    gB.wait_recv()
    top, total = combine(gb_ref, NZ)
    gf_ref[me_q] = top + jnp.log2(total)
    gC = group(me_q, NQ, dev_q)
    gC.start(lambda peer: gf_ref.at[me_q], lambda me: gf_ref.at[me])
    split_rows(2 * strips // 3, strips)
    gC.wait_recv()

    for b in range(NZ):
        k = jnp.exp2(mg_ref[b, 0:1, :] - gf_ref[b])
        k_ref[b] = k
        w_ref[b] = k * jnp.exp(lb_ref[:, b * CB:(b + 1) * CB])

    def row_dots(i, _):
        rows = pl.ds(pl.multiple_of(i * 64, 64), 64)
        acc = jnp.zeros((64, 128), F32)
        for t in range(NT):
            w = w_ref[t // TB, :, (t % TB) * 128:(t % TB + 1) * 128]
            acc += p_ref[rows, t * 128:(t + 1) * 128] * w
        sm_ref[rows, :] = acc
        return 0

    lax.fori_loop(0, S // 64, row_dots, 0)
    for i in range(S // 128):
        rows = slice(i * 128, (i + 1) * 128)
        fr_ref[me_y, :, rows] = jnp.sum(sm_ref[rows, :].T, 0, keepdims=True)
    f2 = group(me_y, NY, dev_y)
    f2.start(lambda peer: fr_ref.at[me_y], lambda me: fr_ref.at[me])
    f2.wait_recv()
    total = add_up(fr_ref, NY)
    scale = jnp.exp(la_ref[...]) / total
    spread(scale)
    x = x_ref[...]
    f_out[...] = jnp.sum(x * x, 0, keepdims=True) / E - (jnp.log2(total) - la2 + lse) / BETA
    for k in range(NY):
        a_ref[k] = scale[:, k * RB:(k + 1) * RB]

    def column_dots(b, _):
        cols = pl.ds(pl.multiple_of(b * CB, CB), CB)

        def step(i, acc):
            rows = pl.ds(pl.multiple_of(i * RS, RS), RS)
            v = jnp.concatenate([vb_ref[rows, :]] * TB, 1)
            return acc + jnp.sum((p_ref[rows, cols] * v).reshape(RS // 8, 8, CB), 0)

        acc = lax.fori_loop(0, S // RS, step, jnp.zeros((8, CB), F32))
        cs_ref[b] = jnp.sum(acc, 0, keepdims=True) * k_ref[b]
        return 0

    lax.fori_loop(0, NZ, column_dots, 0)

    cA = group(me_q, NQ, dev_q)
    cA.start(lambda peer: cs_ref.at[peer], lambda me: ca_ref.at[me])
    ca_ref[me_q] = cs_ref[me_q]

    x1, x2, x3 = split3(x * scale)
    xa_ref[0:E, :] = x1
    xa_ref[E:2 * E, :] = x2
    xa_ref[2 * E:3 * E, :] = x3

    def pulled(first, last):
        def body(b, _):
            cols = pl.ds(pl.multiple_of(b * CB, CB), CB)
            xa = xa_ref[...]
            out = jnp.dot(xa, hi_ref[:, cols], preferred_element_type=F32)
            out = out + jnp.dot(xa, lo_ref[:, cols], preferred_element_type=F32)
            out = (out[0:E] + out[E:2 * E] + out[2 * E:3 * E]) * k_ref[b]
            for t in range(NX):
                for h in range(2):
                    u_ref[t, h, b] = out[h * (E // 2):(h + 1) * (E // 2), t * 128:(t + 1) * 128]
            return 0

        lax.fori_loop(first, last, body, 0)

    pulled(0, NZ // 2)
    cA.wait_recv()
    cb_ref[me_z] = add_up(ca_ref, NQ)
    cB = group(me_z, NZ, dev_z)
    cB.start(lambda peer: cb_ref.at[me_z], lambda me: cb_ref.at[me])
    pulled(NZ // 2, NZ)
    cB.wait_recv()
    d_ref[me_q] = add_up(cb_ref, NZ)
    cC = group(me_q, NQ, dev_q)
    cC.start(lambda peer: d_ref.at[me_q], lambda me: d_ref.at[me])
    u0 = group(me_c, 2, dev_c)
    u0.start(lambda peer: u_ref.at[:, peer], lambda me: r0_ref)
    cC.wait_recv()

    def prep_b(b, _):
        cols = pl.ds(pl.multiple_of(b * CB, CB), CB)
        scale_b = w_ref[b] / d_ref[b]
        y1, y2, y3 = split3(y_ref[:, cols] * scale_b)
        yb_ref[0:E, cols] = y1
        yb_ref[E:2 * E, cols] = y2
        yb_ref[2 * E:3 * E, cols] = y3
        b1, b2, b3 = split3(scale_b)
        row = lax.broadcasted_iota(jnp.int32, (E, CB), 0)
        pick = lambda n, v: jnp.where(row == n, jnp.broadcast_to(v.astype(F32), (E, CB)), 0.0)
        yb_ref[3 * E:4 * E, cols] = (pick(0, b1) + pick(1, b2) + pick(2, b3)).astype(BF16)
        return 0

    lax.fori_loop(0, NZ, prep_b, 0)

    u0.wait_recv()
    for t in range(NX):
        t1_ref[t] = u_ref[t, me_c] + r0_ref[t]
    u1 = group(me_x, NX, dev_x)
    u1.start(lambda peer: t1_ref.at[peer], lambda me: r1_ref.at[me])
    r1_ref[me_x] = t1_ref[me_x]

    sg = group(me_y, NY, dev_y)

    def sg_copy(r):
        return pltpu.make_async_remote_copy(
            src_ref=so_ref.at[r],
            dst_ref=sr_ref.at[me_y],
            send_sem=send_sems.at[sg.base + r],
            recv_sem=recv_sems.at[sg.base + r],
            device_id=dev_y(lax.rem(me_y + 1 + r, NY)),
            device_id_type=MESH,
        )

    def moved(r, _):
        k = lax.rem(me_y + 1 + r, NY)
        rows = pl.ds(pl.multiple_of(k * RB, RB), RB)
        nt = (((1,), (1,)), ((), ()))
        yb = yb_ref[...]
        out = lax.dot_general(hi_ref[rows, :], yb, nt, preferred_element_type=F32)
        out = out + lax.dot_general(lo_ref[rows, :], yb, nt, preferred_element_type=F32)
        out = out.T
        mass = out[3 * E:3 * E + 1] + out[3 * E + 1:3 * E + 2] + out[3 * E + 2:3 * E + 3]
        term = x_ref[:, rows] * mass - (out[0:E] + out[E:2 * E] + out[2 * E:3 * E])
        term = term * a_ref[k]

        @pl.when(r < NY - 1)
        def _():
            so_ref[r] = term
            sg_copy(r).start()

        @pl.when(r == NY - 1)
        def _():
            sr_ref[me_y] = term

        return 0

    lax.fori_loop(0, NY, moved, 0)

    u1.wait_recv()
    for j in range(NZ):
        t2_ref[j] = add_up(r1_ref.at[:, j], NX)
    u2 = group(me_z, NZ, dev_z)
    u2.start(lambda peer: t2_ref.at[peer], lambda me: r2_ref.at[me])
    r2_ref[me_z] = t2_ref[me_z]

    for r in range(NY - 1):
        sg_copy(r).wait_recv()
    sgb_ref[me_y] = add_up(sr_ref, NY)
    ag = group(me_y, NY, dev_y)
    ag.start(lambda peer: sgb_ref.at[me_y], lambda me: sgb_ref.at[me])

    u2.wait_recv()
    r3_ref[me_c] = add_up(r2_ref, NZ)
    u3 = group(me_c, 2, dev_c)
    u3.start(lambda peer: r3_ref.at[me_c], lambda me: r3_ref.at[me])

    for b in range(NZ):
        cols = slice(b * CB, (b + 1) * CB)
        g_out[:, cols] = (LOG2E * lb_ref[:, cols] - gf_ref[b] - jnp.log2(d_ref[b])) / BETA

    u3.wait_recv()
    mine = pl.ds(pl.multiple_of((src // 2) * 128, 128), 128)
    d = d_ref[me_z, :, pl.ds(pl.multiple_of(me_x * 128, 128), 128)]
    total = jnp.concatenate([r3_ref[0], r3_ref[1]], 0)
    term = jnp.exp(lb_ref[:, mine]) * (y_ref[:, mine] - total / d)
    tg_out[...] = jnp.where(me_c == 0, term[:, 0:64], term[:, 64:128])

    ag.wait_recv()
    for k in range(NY):
        sg_out[:, k * RB:(k + 1) * RB] = sgb_ref[k]

    for exchange in (f1, gA, gB, gC, f2, cA, cB, cC, u0, u1, u2, ag, u3):
        exchange.wait_send()
    for r in range(NY - 1):
        sg_copy(r).wait_send()


def local(dims, x, y, la, lb):
    NX, NZ, NY = dims
    NQ = 2 * NX
    E, S = x.shape
    T = y.shape[1]
    CB = T // NZ
    RB = S // NY
    n_sems = 3 * (NY - 1) + 4 * (NQ - 1) + 2 * (NZ - 1) + (NY - 1) + 2 + (NX - 1) + (NZ - 1)
    H = E // 2
    vmem = lambda shape, dtype=F32: pltpu.VMEM(shape, dtype)
    out = pl.pallas_call(
        functools.partial(kernel, dims),
        out_shape=(
            jax.ShapeDtypeStruct((1, S), F32),
            jax.ShapeDtypeStruct((1, T), F32),
            jax.ShapeDtypeStruct((E, S), F32),
            jax.ShapeDtypeStruct((E, 64), F32),
        ),
        in_specs=[pl.BlockSpec(memory_space=pltpu.VMEM)] * 4,
        out_specs=[pl.BlockSpec(memory_space=pltpu.VMEM)] * 4,
        scratch_shapes=[
            vmem((S, T)), vmem((S, T), BF16), vmem((S, T), BF16),
            vmem((S, 8 * E), BF16), vmem((8 * E, T), BF16),
            vmem((S, 128)), vmem((S, 128)), vmem((S, 128)),
            vmem((NY, 2, S)), vmem((NY, 1, S)),
            vmem((NQ, 2, CB)), vmem((NQ, 2, CB)), vmem((NZ, 2, CB)), vmem((NQ, 1, CB)),
            vmem((NQ, 1, CB)), vmem((NQ, 1, CB)),
            vmem((NQ, 1, CB)), vmem((NQ, 1, CB)), vmem((NZ, 1, CB)), vmem((NQ, 1, CB)),
            vmem((NY, 1, RB)), vmem((3 * E, S), BF16), vmem((4 * E, T), BF16),
            vmem((NX, 2, NZ, H, 128)), vmem((NX, NZ, H, 128)), vmem((NX, NZ, H, 128)),
            vmem((NX, NZ, H, 128)), vmem((NZ, H, 128)), vmem((NZ, H, 128)), vmem((2, H, 128)),
            vmem((NY - 1, E, RB)), vmem((NY, E, RB)), vmem((NY, E, RB)),
            pltpu.SemaphoreType.DMA((n_sems,)), pltpu.SemaphoreType.DMA((n_sems,)),
        ],
        compiler_params=pltpu.CompilerParams(
            collective_id=0, has_side_effects=True, vmem_limit_bytes=56 * 1024 * 1024
        ),
        cost_estimate=pl.CostEstimate(
            flops=2 * S * T * (8 + 8 + 8) * E, bytes_accessed=4 * (E * (S + T) * 2), transcendentals=2 * S * T
        ),
        name="sinkhorn",
    )(x, y, la[None, :], lb[None, :])
    f, g, sg, tg = out
    return f[0], g[0], sg, tg[:, None, :]


def solution(mesh):
    n_src, n_tgt = mesh.shape["src"], mesh.shape["tgt"]
    n_x = int(round((n_src // 4) ** 0.5))
    dims = (n_x, n_src // (2 * n_x), n_tgt)
    placed = (P(None, "src"), P(None, "tgt"), P("src"), P("tgt"))
    return jax.shard_map(
        functools.partial(local, dims),
        mesh=mesh,
        in_specs=placed,
        out_specs=(P("src"), P("tgt"), P(None, "src"), P(None, "tgt", "src")),
        check_vma=False,
    )
```

```python
import functools

import jax
import jax.numpy as jnp
import numpy as np
from jax import lax
from jax.experimental import pallas as pl
from jax.experimental.pallas import tpu as pltpu
from jax.sharding import PartitionSpec as P

EPSILON = 0.05
LOG2E = float(np.log2(np.e))
BETA = LOG2E / EPSILON
MESH = pl.DeviceIdType.MESH
F32 = jnp.float32
BF16 = jnp.bfloat16
RS = 128
RC = 64
L = 128


def split3(a):
    hi = a.astype(BF16)
    rest = a - hi.astype(F32)
    mid = rest.astype(BF16)
    lo = (rest - mid.astype(F32)).astype(BF16)
    return hi, mid, lo


def ds(start, size):
    return pl.ds(pl.multiple_of(start, size), size)


def lse2(ref, n):
    top = ref[0]
    for j in range(1, n):
        top = jnp.maximum(top, ref[j])
    total = jnp.exp2(ref[0] - top)
    for j in range(1, n):
        total = total + jnp.exp2(ref[j] - top)
    return top + jnp.log2(total)


def add_up(ref, n):
    total = ref[0]
    for j in range(1, n):
        total = total + ref[j]
    return total


class Sends:
    def __init__(self, send_sems, recv_sems):
        self.send_sems, self.recv_sems = send_sems, recv_sems
        self.taken = 0
        self.live = []

    def reserve(self, n):
        self.taken += n
        return self.taken - n

    def copy(self, src, dst, send, recv, device):
        return pltpu.make_async_remote_copy(
            src_ref=src,
            dst_ref=dst,
            send_sem=self.send_sems.at[send],
            recv_sem=self.recv_sems.at[recv],
            device_id=device,
            device_id_type=MESH,
        )

    def exchange(self, src, dst, me, n, device):
        base = self.reserve(n - 1)
        copies = []
        for r in range(1, n):
            peer = lax.rem(me + r, n)
            copies.append(self.copy(src(peer), dst, base + r - 1, base + r - 1, device(peer)))
        for copy in copies:
            copy.start()
        self.live += copies
        return copies


def arrived(copies):
    for copy in copies:
        copy.wait_recv()


def kernel(dims, x_ref, y_ref, la_ref, lb_ref,
           f_out, g_out, sg_out, tg_out,
           p_ref, hi_ref, lo_ref, xk_ref, yk_ref, mx_ref, sm_ref, vb_ref, cm_ref, mf_ref,
           xs_ref, las_ref, tmp_ref, fm_ref, fr_ref, gm_ref, gx_ref, gz_ref, k_ref, w_ref,
           a_ref, xa_ref, yb_ref, cx_ref, cz_ref, d_ref, gs_ref,
           u_ref, r1_ref, t2_ref, r2_ref, tile_ref, so_ref, sc_ref, sy_ref, sr_ref, sgb_ref,
           send_sems, recv_sems):
    NX, NZ, NY = dims
    NQ = 2 * NX
    E, S = x_ref.shape
    T = y_ref.shape[1]
    T2, S2 = T // 2, 2 * S
    HZ = NZ // 2
    CB = NX * L
    RB = S // NY
    NH = NY // 2
    NT, NR, SR = T2 // L, S2 // L, S // L

    src = lax.axis_index("src")
    me_y = lax.axis_index("tgt")
    me_z = src // NQ
    me_q = lax.rem(src, NQ)
    me_x = me_q // 2
    me_c = lax.rem(me_q, 2)
    other = 1 - me_c
    me_f = me_y * 2 + me_c
    chip = src - me_c

    dev_f = lambda j: {"src": chip + lax.rem(j, 2), "tgt": j // 2}
    dev_y = lambda j: {"tgt": j}
    dev_z = lambda j: {"src": j * NQ + me_q}
    dev_x = lambda j: {"src": me_z * NQ + j * 2 + me_c}
    partner = {"src": chip + other}

    sends = Sends(send_sems, recv_sems)
    exchange = sends.exchange

    barrier = pltpu.get_barrier_semaphore()
    greeted = 0
    for me, n, device in ((me_f, 2 * NY, dev_f), (me_x, NX, dev_x), (me_z, NZ, dev_z)):
        for r in range(1, n):
            pl.semaphore_signal(barrier, inc=1, device_id=device(lax.rem(me + r, n)), device_id_type=MESH)
            greeted += 1

    def prep_y(b, _):
        cols = ds(b * CB, CB)
        y = y_ref[:, ds(me_c * T2 + b * CB, CB)]
        y1, y2, y3 = split3(y)
        for n, part in enumerate((y1, y2, y1, y3, y2, y1)):
            yk_ref[n * E:(n + 1) * E, cols] = part
        lb = jnp.concatenate([lb_ref[pl.ds(me_c * NT + b * NX + t, 1), :] for t in range(NX)], 1)
        u = LOG2E * lb - (BETA / E) * jnp.sum(y * y, 0, keepdims=True)
        u1, u2, u3 = split3(u)
        row = lax.broadcasted_iota(jnp.int32, (16, CB), 0)
        pick = lambda n, v: jnp.where(row == n, jnp.broadcast_to(v.astype(F32), (16, CB)), 0.0)
        yk_ref[6 * E:6 * E + 16, cols] = (pick(0, u1) + pick(1, u2) + pick(2, u3)).astype(BF16)
        yk_ref[6 * E + 16:8 * E, cols] = jnp.zeros((2 * E - 16, CB), BF16)
        return 0

    lax.fori_loop(0, HZ, prep_y, 0)

    lane = lax.broadcasted_iota(jnp.int32, (L, L), 1)
    left = lane < E

    def prep_x(h):
        def body(i, _):
            rows = ds(h * S + i * L, L)
            x = xs_ref[h, :, ds(i * L, L)] * (2.0 * BETA / E)
            x1, x2, x3 = (v.astype(F32) for v in split3(jnp.concatenate([x, x], 0).T))
            xk_ref[rows, 0:128] = x1.astype(BF16)
            xk_ref[rows, 128:256] = jnp.where(left, x2, x1).astype(BF16)
            xk_ref[rows, 256:384] = jnp.where(left, x2, x3).astype(BF16)
            xk_ref[rows, 384:512] = jnp.where(lane < 3, 1.0, 0.0).astype(BF16)
            mx_ref[rows, :] = jnp.full((L, L), -3e38, F32)
            sm_ref[rows, :] = jnp.zeros((L, L), F32)
            return 0

        lax.fori_loop(0, SR, body, 0)

    W2 = T2 // 2

    def scores(h, b):
        yk = yk_ref[:, b * W2:(b + 1) * W2]
        for i in range(S // RS):
            rows = ds(h * S + i * RS, RS)
            s = jnp.dot(xk_ref[rows, :], yk, preferred_element_type=F32)
            p_ref[rows, b * W2:(b + 1) * W2] = s
            old = mx_ref[rows, :]
            m = old
            for t in range(W2 // L):
                m = jnp.maximum(m, s[:, t * L:(t + 1) * L])
            acc = sm_ref[rows, :] * jnp.exp2(old - m)
            for t in range(W2 // L):
                acc = acc + jnp.exp2(s[:, t * L:(t + 1) * L] - m)
            mx_ref[rows, :] = m
            sm_ref[rows, :] = acc

    xs_ref[me_c] = x_ref[...]
    las_ref[me_c] = la_ref[...]
    prep_x(me_c)
    scores(me_c, 0)
    pl.semaphore_wait(barrier, greeted)
    base = sends.reserve(2)
    swap = [
        sends.copy(x_ref, xs_ref.at[me_c], base, base, partner),
        sends.copy(la_ref, las_ref.at[me_c], base + 1, base + 1, partner),
    ]
    for copy in swap:
        copy.start()
    sends.live += swap
    scores(me_c, 1)
    arrived(swap)
    prep_x(other)
    scores(other, 0)
    scores(other, 1)

    for i in range(NR):
        rows = slice(i * L, (i + 1) * L)
        m = mx_ref[rows, :].T
        top = jnp.max(m, 0, keepdims=True)
        tmp_ref[0, i:i + 1, :] = top
        tmp_ref[1, i:i + 1, :] = jnp.sum(sm_ref[rows, :].T * jnp.exp2(m - top), 0, keepdims=True)
    fm_ref[me_f] = tmp_ref[0] + jnp.log2(tmp_ref[1])
    f1 = exchange(lambda peer: fm_ref.at[me_f], fm_ref.at[me_f], me_f, 2 * NY, dev_f)

    la = jnp.concatenate([las_ref[0], las_ref[1]], 0)
    la2 = LOG2E * la

    def spread(a):
        for i in range(NR):
            vb_ref[i * L:(i + 1) * L, :] = jnp.broadcast_to(a[i:i + 1, :], (L, L)).T

    arrived(f1)
    lse = lse2(fm_ref, 2 * NY)
    spread(la2 - lse)

    def columns(b, _):
        cols = ds(b * CB, CB)

        def step(i, carry):
            old, acc = carry
            rows = ds(i * RC, RC)
            v = vb_ref[rows, :]
            t = (p_ref[rows, cols] + jnp.concatenate([v] * NX, 1)).reshape(RC // 8, 8, CB)
            m = jnp.maximum(old, jnp.max(t, 0))
            e = jnp.exp2(t - m)
            p_ref[rows, cols] = e.reshape(RC, CB)
            cm_ref[i, :, cols] = m
            return m, acc * jnp.exp2(old - m) + jnp.sum(e, 0)

        m, acc = lax.fori_loop(
            0, S2 // RC, step, (jnp.full((8, CB), -3e38, F32), jnp.zeros((8, CB), F32))
        )
        top = jnp.max(m, 0, keepdims=True)
        total = jnp.sum(acc * jnp.exp2(m - top), 0, keepdims=True)
        mf_ref[:, cols] = top
        for t in range(NX):
            tmp_ref[0, pl.ds(b * NX + t, 1), :] = top[:, t * L:(t + 1) * L]
            tmp_ref[1, pl.ds(b * NX + t, 1), :] = total[:, t * L:(t + 1) * L]
        return 0

    lax.fori_loop(0, HZ, columns, 0)

    m_col = tmp_ref[0, 0:NT]
    gx_ref[me_x] = m_col + jnp.log2(tmp_ref[1, 0:NT])
    gX = exchange(lambda peer: gx_ref.at[me_x], gx_ref.at[me_x], me_x, NX, dev_x)

    def settle(first, last):
        def body(i, _):
            rows = ds(i * RC, RC)
            for t in range(T2 // CB):
                lanes = slice(t * CB, (t + 1) * CB)
                fix = jnp.exp2(cm_ref[i, :, lanes] - mf_ref[:, lanes])
                e = (p_ref[rows, lanes].reshape(RC // 8, 8, CB) * fix).reshape(RC, CB)
                p_ref[rows, lanes] = e
                hi = e.astype(BF16)
                hi_ref[rows, lanes] = hi
                lo_ref[rows, lanes] = (e - hi.astype(F32)).astype(BF16)
            return 0

        lax.fori_loop(first, last, body, 0)

    steps = S2 // RC
    settle(0, steps // 2)
    arrived(gX)
    gz_ref[me_z] = lse2(gx_ref, NX)
    gZ = exchange(lambda peer: gz_ref.at[me_z], gz_ref.at[me_z], me_z, NZ, dev_z)
    settle(steps // 2, steps)
    arrived(gZ)
    g_lse = lse2(gz_ref, NZ)
    k = jnp.exp2(m_col - g_lse)
    k_ref[...] = k
    b_mine = lb_ref[ds(me_c * NT, NT), :]
    w_ref[...] = k * jnp.exp(b_mine)

    def row_dots(i, _):
        rows = ds(i * 64, 64)
        acc = jnp.zeros((64, L), F32)
        for t in range(NT):
            acc += p_ref[rows, t * L:(t + 1) * L] * w_ref[t:t + 1, :]
        sm_ref[rows, :] = acc
        return 0

    lax.fori_loop(0, S2 // 64, row_dots, 0)
    for i in range(NR):
        fr_ref[me_f, i:i + 1, :] = jnp.sum(sm_ref[i * L:(i + 1) * L, :].T, 0, keepdims=True)
    f2 = exchange(lambda peer: fr_ref.at[me_f], fr_ref.at[me_f], me_f, 2 * NY, dev_f)
    arrived(f2)
    total = add_up(fr_ref, 2 * NY)
    scale = jnp.exp(la) / total
    a_ref[...] = scale
    spread(scale)

    def column_dots(b, _):
        cols = ds(b * CB, CB)

        def step(i, acc):
            rows = ds(i * RS, RS)
            v = jnp.concatenate([vb_ref[rows, :]] * NX, 1)
            return acc + jnp.sum((p_ref[rows, cols] * v).reshape(RS // 8, 8, CB), 0)

        acc = lax.fori_loop(0, S2 // RS, step, jnp.zeros((8, CB), F32))
        acc = jnp.sum(acc, 0, keepdims=True)
        for t in range(NX):
            tmp_ref[0, pl.ds(b * NX + t, 1), :] = acc[:, t * L:(t + 1) * L]
        return 0

    lax.fori_loop(0, HZ, column_dots, 0)
    cx_ref[me_x] = tmp_ref[0, 0:NT] * k_ref[...]
    cX = exchange(lambda peer: cx_ref.at[me_x], cx_ref.at[me_x], me_x, NX, dev_x)

    mine = lambda v: jnp.where(me_c == 0, v[0:SR], v[SR:NR])
    potential = (jnp.log2(total) - la2 + lse) / BETA
    for i in range(SR):
        x = x_ref[:, i * L:(i + 1) * L]
        tmp_ref[1, i:i + 1, :] = jnp.sum(x * x, 0, keepdims=True) / E
    f_out[...] = tmp_ref[1, 0:SR] - mine(potential)

    for h in range(2):
        for i in range(SR):
            n = h * SR + i
            parts = split3(xs_ref[h, :, i * L:(i + 1) * L] * scale[n:n + 1, :])
            for j, part in enumerate(parts):
                xa_ref[j * E:(j + 1) * E, n * L:(n + 1) * L] = part

    def pulled(first, last):
        def body(b, _):
            cols = ds(b * CB, CB)
            out = jnp.dot(xa_ref[...], hi_ref[:, cols], preferred_element_type=F32)
            low = jnp.dot(xa_ref[0:2 * E, :], lo_ref[:, cols], preferred_element_type=F32)
            out = out[0:E] + out[E:2 * E] + out[2 * E:3 * E] + low[0:E] + low[E:2 * E]
            for t in range(NX):
                u_ref[t, b] = out[:, t * L:(t + 1) * L] * k_ref[pl.ds(b * NX + t, 1), :]
            return 0

        lax.fori_loop(first, last, body, 0)

    pulled(0, HZ // 2)
    arrived(cX)
    cz_ref[me_z] = add_up(cx_ref, NX)
    cZ = exchange(lambda peer: cz_ref.at[me_z], cz_ref.at[me_z], me_z, NZ, dev_z)
    pulled(HZ // 2, HZ)
    uX = exchange(lambda peer: u_ref.at[peer], r1_ref.at[me_x], me_x, NX, dev_x)
    arrived(cZ)
    d = add_up(cz_ref, NZ)
    d_ref[...] = d
    tmp_ref[0, 0:NT] = w_ref[...] / d

    def prep_b(b, _):
        cols = ds(b * CB, CB)
        right = jnp.concatenate([tmp_ref[0, pl.ds(b * NX + t, 1), :] for t in range(NX)], 1)
        for j, part in enumerate(split3(y_ref[:, ds(me_c * T2 + b * CB, CB)] * right)):
            yb_ref[j * E:(j + 1) * E, cols] = part
        b1, b2, b3 = split3(right)
        row = lax.broadcasted_iota(jnp.int32, (E, CB), 0)
        pick = lambda n, v: jnp.where(row == n, jnp.broadcast_to(v.astype(F32), (E, CB)), 0.0)
        yb_ref[3 * E:4 * E, cols] = (pick(0, b1) + pick(1, b2) + pick(2, b3)).astype(BF16)
        return 0

    lax.fori_loop(0, HZ, prep_b, 0)

    gs_ref[me_c] = (LOG2E * b_mine - g_lse - jnp.log2(d)) / BETA
    gC = exchange(lambda peer: gs_ref.at[me_c], gs_ref.at[me_c], me_c, 2, lambda j: {"src": chip + j})

    core_base = sends.reserve(NH)
    tgt_base = sends.reserve(NY)

    def core_copy(q):
        return sends.copy(so_ref.at[q], sc_ref.at[q], core_base + q, core_base + q, partner)

    def tgt_copy(owner, sender):
        return sends.copy(sy_ref.at[owner], sr_ref.at[sender], tgt_base + owner, tgt_base + sender, dev_y(owner))

    def moved(r, _):
        own = r >= NH
        h = jnp.where(own, me_c, other)
        q = jnp.where(own, lax.rem(r - NH + me_y // 2 + 1 + NH, NH), r)
        rows = ds(h * S + q * (2 * RB), 2 * RB)
        nt = (((1,), (1,)), ((), ()))
        out = lax.dot_general(hi_ref[rows, :], yb_ref[...], nt, preferred_element_type=F32)
        out = out + lax.dot_general(lo_ref[rows, :], yb_ref[...], nt, preferred_element_type=F32)
        out = out.T
        mass = out[3 * E:3 * E + 1] + out[3 * E + 1:3 * E + 2] + out[3 * E + 2:3 * E + 3]
        term = xs_ref[h, :, ds(q * (2 * RB), 2 * RB)] * mass - (out[0:E] + out[E:2 * E] + out[2 * E:3 * E])
        first = h * SR + q * (2 * RB // L)
        term = term * jnp.concatenate([a_ref[pl.ds(first + t, 1), :] for t in range(2 * RB // L)], 1)

        @pl.when(r < NH)
        def _():
            so_ref[q] = term
            core_copy(q).start()

        @pl.when(r >= NH)
        def _():
            core_copy(q).wait_recv()
            both = term + sc_ref[q]
            for e in range(2):
                owner = 2 * q + e
                part = both[:, e * RB:(e + 1) * RB]

                @pl.when(owner == me_y)
                def _():
                    sr_ref[me_y] = part

                @pl.when(owner != me_y)
                def _():
                    sy_ref[owner] = part
                    tgt_copy(owner, me_y).start()

        return 0

    lax.fori_loop(0, 2 * NH, moved, 0)

    arrived(uX)
    for j in range(HZ):
        total = u_ref[me_x, j]
        for r in range(1, NX):
            total = total + r1_ref[lax.rem(me_x + r, NX), j]
        t2_ref[j] = total
    z_base = sends.reserve(NZ)
    first_z = me_c * HZ
    holds = me_z // HZ == me_c

    def z_copy(j, sender):
        return sends.copy(t2_ref.at[j], r2_ref.at[sender], z_base + j, z_base + sender, dev_z(first_z + j))

    for j in range(HZ):
        @pl.when(first_z + j != me_z)
        def _():
            z_copy(j, me_z).start()

    for j in range(NY):
        @pl.when(j != me_y)
        def _():
            tgt_copy(me_y, j).wait_recv()

    sgb_ref[me_y] = add_up(sr_ref, NY)
    sY = exchange(lambda peer: sgb_ref.at[me_y], sgb_ref.at[me_y], me_y, NY, dev_y)

    tile_base = sends.reserve(1)
    tile_copy = sends.copy(tile_ref, tile_ref, tile_base, tile_base, partner)

    @pl.when(holds)
    def _():
        for j in range(NZ):
            @pl.when(j != me_z)
            def _():
                z_copy(0, j).wait_recv()

        total = t2_ref[me_z - first_z]
        for r in range(1, NZ):
            total = total + r2_ref[lax.rem(me_z + r, NZ)]
        here = (me_z - first_z) * NX + me_x
        b = jnp.exp(lb_ref[pl.ds(me_z * NX + me_x, 1), :])
        y = y_ref[:, ds((me_z * NX + me_x) * L, L)]
        tile_ref[...] = b * (y - total / d_ref[pl.ds(here, 1), :])
        tile_copy.start()

    @pl.when(jnp.logical_not(holds))
    def _():
        tile_copy.wait_recv()

    tile = tile_ref[...]
    tg_out[...] = jnp.where(me_c == 0, tile[:, 0:E], tile[:, E:2 * E])

    arrived(gC)
    g_out[0:NT] = gs_ref[0]
    g_out[NT:2 * NT] = gs_ref[1]

    arrived(sY)
    for j in range(NY):
        sg_out[:, j * RB:(j + 1) * RB] = sgb_ref[j]

    for copy in sends.live:
        copy.wait_send()
    for q in range(NH):
        core_copy(q).wait_send()
    for j in range(NY):
        @pl.when(j != me_y)
        def _():
            tgt_copy(j, me_y).wait_send()
    for j in range(HZ):
        @pl.when(first_z + j != me_z)
        def _():
            z_copy(j, me_z).wait_send()

    @pl.when(holds)
    def _():
        tile_copy.wait_send()


def local(dims, x, y, la, lb):
    NX, NZ, NY = dims
    E, S = x.shape
    T = y.shape[1]
    S2, T2 = 2 * S, T // 2
    HZ, NH, RB = NZ // 2, NY // 2, S // NY
    NT, NR, SR = T2 // L, S2 // L, S // L
    n_sems = 2 + 2 * (2 * NY - 1) + 3 * (NX - 1) + 2 * (NZ - 1) + 1 + NH + NY + NZ + (NY - 1) + 1
    big = max(NT, NR)
    vmem = lambda shape, dtype=F32: pltpu.VMEM(shape, dtype)
    f, g, sg, tg = pl.pallas_call(
        functools.partial(kernel, dims),
        out_shape=(
            jax.ShapeDtypeStruct((SR, L), F32),
            jax.ShapeDtypeStruct((2 * NT, L), F32),
            jax.ShapeDtypeStruct((E, S), F32),
            jax.ShapeDtypeStruct((E, 64), F32),
        ),
        in_specs=[pl.BlockSpec(memory_space=pltpu.VMEM)] * 4,
        out_specs=[pl.BlockSpec(memory_space=pltpu.VMEM)] * 4,
        scratch_shapes=[
            vmem((S2, T2)), vmem((S2, T2), BF16), vmem((S2, T2), BF16),
            vmem((S2, 8 * E), BF16), vmem((8 * E, T2), BF16),
            vmem((S2, L)), vmem((S2, L)), vmem((S2, L)),
            vmem((S2 // RC, 8, T2)), vmem((1, T2)),
            vmem((2, E, S)), vmem((2, SR, L)), vmem((2, big, L)),
            vmem((2 * NY, NR, L)), vmem((2 * NY, NR, L)),
            vmem((NX, NT, L)), vmem((NX, NT, L)), vmem((NZ, NT, L)), vmem((NT, L)), vmem((NT, L)),
            vmem((NR, L)), vmem((3 * E, S2), BF16), vmem((4 * E, T2), BF16),
            vmem((NX, NT, L)), vmem((NZ, NT, L)), vmem((NT, L)), vmem((2, NT, L)),
            vmem((NX, HZ, E, L)), vmem((NX, HZ, E, L)), vmem((HZ, E, L)), vmem((NZ, E, L)), vmem((E, L)),
            vmem((NH, E, 2 * RB)), vmem((NH, E, 2 * RB)),
            vmem((NY, E, RB)), vmem((NY, E, RB)), vmem((NY, E, RB)),
            pltpu.SemaphoreType.DMA((n_sems,)), pltpu.SemaphoreType.DMA((n_sems,)),
        ],
        compiler_params=pltpu.CompilerParams(
            collective_id=0, has_side_effects=True, vmem_limit_bytes=58 * 1024 * 1024
        ),
        cost_estimate=pl.CostEstimate(
            flops=2 * S2 * T2 * (8 + 5 + 8) * E, bytes_accessed=8 * E * (S + T), transcendentals=2 * S2 * T2
        ),
        name="sinkhorn",
    )(x, y, la.reshape(SR, L), lb.reshape(2 * NT, L))
    return f.reshape(S), g.reshape(T), sg, tg[:, None, :]


def solution(mesh):
    n_src, n_tgt = mesh.shape["src"], mesh.shape["tgt"]
    n_x = int(round((n_src // 4) ** 0.5))
    dims = (n_x, n_src // (2 * n_x), n_tgt)
    placed = (P(None, "src"), P(None, "tgt"), P("src"), P("tgt"))
    return jax.shard_map(
        functools.partial(local, dims),
        mesh=mesh,
        in_specs=placed,
        out_specs=(P("src"), P("tgt"), P(None, "src"), P(None, "tgt", "src")),
        check_vma=False,
    )
```

```python
import functools

import jax
import jax.numpy as jnp
import numpy as np
from jax import lax
from jax.experimental import pallas as pl
from jax.experimental.pallas import tpu as pltpu
from jax.sharding import PartitionSpec as P

EPSILON = 0.05
LOG2E = float(np.log2(np.e))
BETA = LOG2E / EPSILON
MESH = pl.DeviceIdType.MESH
F32 = jnp.float32
BF16 = jnp.bfloat16
RS = 128
RC = 64
L = 128


def split3(a):
    hi = a.astype(BF16)
    rest = a - hi.astype(F32)
    mid = rest.astype(BF16)
    lo = (rest - mid.astype(F32)).astype(BF16)
    return hi, mid, lo


def ds(start, size):
    return pl.ds(pl.multiple_of(start, size), size)


def lse2(ref, n):
    top = ref[0]
    for j in range(1, n):
        top = jnp.maximum(top, ref[j])
    total = jnp.exp2(ref[0] - top)
    for j in range(1, n):
        total = total + jnp.exp2(ref[j] - top)
    return top + jnp.log2(total)


def add_up(ref, n):
    total = ref[0]
    for j in range(1, n):
        total = total + ref[j]
    return total


class Sends:
    def __init__(self, send_sems, recv_sems):
        self.send_sems, self.recv_sems = send_sems, recv_sems
        self.taken = 0
        self.live = []

    def reserve(self, n):
        self.taken += n
        return self.taken - n

    def copy(self, src, dst, send, recv, device):
        return pltpu.make_async_remote_copy(
            src_ref=src,
            dst_ref=dst,
            send_sem=self.send_sems.at[send],
            recv_sem=self.recv_sems.at[recv],
            device_id=device,
            device_id_type=MESH,
        )

    def exchange(self, src, dst, me, n, device):
        base = self.reserve(n - 1)
        copies = []
        for r in range(1, n):
            peer = lax.rem(me + r, n)
            copies.append(self.copy(src(peer), dst, base + r - 1, base + r - 1, device(peer)))
        for copy in copies:
            copy.start()
        self.live += copies
        return copies


def arrived(copies):
    for copy in copies:
        copy.wait_recv()


def kernel(dims, x_ref, y_hbm, la_ref, lb_ref,
           f_out, g_out, sg_out, tg_out,
           p_ref, hi_ref, lo_ref, xk_ref, yk_ref, mx_ref, sm_ref, vb_ref, cm_ref, mf_ref,
           xs_ref, las_ref, tmp_ref, run_ref, fc_ref, fm_ref, frc_ref, fr_ref, gm_ref, gx_ref, gz_ref, k_ref, w_ref,
           a_ref, xa_ref, yb_ref, cx_ref, cz_ref, d_ref, gs_ref,
           u_ref, r1_ref, t2_ref, r2_ref, tile_ref, so_ref, sc_ref, sy_ref, sr_ref, sgb_ref,
           y_ref, send_sems, recv_sems, y_sems):
    NX, NZ, NY = dims
    NQ = 2 * NX
    E, S = x_ref.shape
    T = y_hbm.shape[1]
    T2, S2 = T // 2, 2 * S
    HZ = NZ // 2
    CB = NX * L
    RB = S // NY
    NT, NR, SR = T2 // L, S2 // L, S // L

    src = lax.axis_index("src")
    me_y = lax.axis_index("tgt")
    me_z = src // NQ
    me_q = lax.rem(src, NQ)
    me_x = me_q // 2
    me_c = lax.rem(me_q, 2)
    other = 1 - me_c
    chip = src - me_c

    dev_c = lambda j: {"src": chip + j}
    dev_y = lambda j: {"tgt": j}
    dev_z = lambda j: {"src": j * NQ + me_q}
    dev_x = lambda j: {"src": me_z * NQ + j * 2 + me_c}
    partner = {"src": chip + other}

    sends = Sends(send_sems, recv_sems)
    exchange = sends.exchange

    loads = [
        pltpu.make_async_copy(
            y_hbm.at[:, ds(me_c * T2 + b * CB, CB)], y_ref.at[:, b * CB:(b + 1) * CB], y_sems.at[b]
        )
        for b in range(HZ)
    ]
    for load in loads:
        load.start()

    barrier = pltpu.get_barrier_semaphore()
    greeted = 0
    for me, n, device in ((me_c, 2, dev_c), (me_y, NY, dev_y), (me_x, NX, dev_x), (me_z, NZ, dev_z)):
        for r in range(1, n):
            pl.semaphore_signal(barrier, inc=1, device_id=device(lax.rem(me + r, n)), device_id_type=MESH)
            greeted += 1

    def prep_y(b, _):
        cols = ds(b * CB, CB)
        y = y_ref[:, cols]
        y1, y2, y3 = split3(y)
        for n, part in enumerate((y1, y2, y1, y3, y2, y1)):
            yk_ref[n * E:(n + 1) * E, cols] = part
        lb = jnp.concatenate([lb_ref[pl.ds(me_c * NT + b * NX + t, 1), :] for t in range(NX)], 1)
        u = LOG2E * lb - (BETA / E) * jnp.sum(y * y, 0, keepdims=True)
        u1, u2, u3 = split3(u)
        row = lax.broadcasted_iota(jnp.int32, (16, CB), 0)
        pick = lambda n, v: jnp.where(row == n, jnp.broadcast_to(v.astype(F32), (16, CB)), 0.0)
        yk_ref[6 * E:6 * E + 16, cols] = (pick(0, u1) + pick(1, u2) + pick(2, u3)).astype(BF16)
        yk_ref[6 * E + 16:8 * E, cols] = jnp.zeros((2 * E - 16, CB), BF16)
        return 0


    lane = lax.broadcasted_iota(jnp.int32, (L, L), 1)
    left = lane < E

    def prep_x(h):
        def body(i, _):
            rows = ds(h * S + i * L, L)
            x = xs_ref[h, :, ds(i * L, L)] * (2.0 * BETA / E)
            x1, x2, x3 = (v.astype(F32) for v in split3(jnp.concatenate([x, x], 0).T))
            xk_ref[rows, 0:128] = x1.astype(BF16)
            xk_ref[rows, 128:256] = jnp.where(left, x2, x1).astype(BF16)
            xk_ref[rows, 256:384] = jnp.where(left, x2, x3).astype(BF16)
            xk_ref[rows, 384:512] = jnp.where(lane < 3, 1.0, 0.0).astype(BF16)
            mx_ref[rows, :] = jnp.full((L, L), -3e38, F32)
            sm_ref[rows, :] = jnp.zeros((L, L), F32)
            return 0

        lax.fori_loop(0, SR, body, 0)

    W2 = T2 // 2

    def scores(h, b):
        yk = yk_ref[:, b * W2:(b + 1) * W2]
        for i in range(S // RS):
            rows = ds(h * S + i * RS, RS)
            s = jnp.dot(xk_ref[rows, :], yk, preferred_element_type=F32)
            p_ref[rows, b * W2:(b + 1) * W2] = s
            old = mx_ref[rows, :]
            m = old
            for t in range(W2 // L):
                m = jnp.maximum(m, s[:, t * L:(t + 1) * L])
            acc = sm_ref[rows, :] * jnp.exp2(old - m)
            for t in range(W2 // L):
                acc = acc + jnp.exp2(s[:, t * L:(t + 1) * L] - m)
            mx_ref[rows, :] = m
            sm_ref[rows, :] = acc

    xs_ref[me_c] = x_ref[...]
    las_ref[me_c] = la_ref[...]
    prep_x(me_c)
    for load in loads:
        load.wait()
    lax.fori_loop(0, HZ, prep_y, 0)
    scores(me_c, 0)
    pl.semaphore_wait(barrier, greeted)
    base = sends.reserve(2)
    swap = [
        sends.copy(x_ref, xs_ref.at[me_c], base, base, partner),
        sends.copy(la_ref, las_ref.at[me_c], base + 1, base + 1, partner),
    ]
    for copy in swap:
        copy.start()
    sends.live += swap
    scores(me_c, 1)
    arrived(swap)
    prep_x(other)
    scores(other, 0)
    scores(other, 1)

    for i in range(NR):
        rows = slice(i * L, (i + 1) * L)
        m = mx_ref[rows, :].T
        top = jnp.max(m, 0, keepdims=True)
        tmp_ref[0, i:i + 1, :] = top
        tmp_ref[1, i:i + 1, :] = jnp.sum(sm_ref[rows, :].T * jnp.exp2(m - top), 0, keepdims=True)
    fc_ref[me_c] = tmp_ref[0] + jnp.log2(tmp_ref[1])
    f1c = exchange(lambda peer: fc_ref.at[me_c], fc_ref.at[me_c], me_c, 2, dev_c)

    la = jnp.concatenate([las_ref[0], las_ref[1]], 0)
    la2 = LOG2E * la

    def spread(a):
        for i in range(NR):
            vb_ref[i * L:(i + 1) * L, :] = jnp.broadcast_to(a[i:i + 1, :], (L, L)).T

    arrived(f1c)
    fm_ref[me_y] = lse2(fc_ref, 2)
    f1 = exchange(lambda peer: fm_ref.at[me_y], fm_ref.at[me_y], me_y, NY, dev_y)
    run_ref[0] = jnp.full((8, T2), -3e38, F32)
    run_ref[1] = jnp.zeros((8, T2), F32)
    arrived(f1)
    lse = lse2(fm_ref, NY)
    spread(la2 - lse)

    def columns(i, _):
        rows = ds(i * RC, RC)
        v = jnp.concatenate([vb_ref[rows, :]] * NX, 1)
        for b in range(HZ):
            cols = slice(b * CB, (b + 1) * CB)
            t = (p_ref[rows, cols] + v).reshape(RC // 8, 8, CB)
            old = run_ref[0, :, cols]
            m = jnp.maximum(old, jnp.max(t, 0))
            e = jnp.exp2(t - m)
            p_ref[rows, cols] = e.reshape(RC, CB)
            cm_ref[i, :, cols] = m
            run_ref[0, :, cols] = m
            run_ref[1, :, cols] = run_ref[1, :, cols] * jnp.exp2(old - m) + jnp.sum(e, 0)
        return 0

    lax.fori_loop(0, S2 // RC, columns, 0)
    for t in range(NT):
        cols = slice(t * L, (t + 1) * L)
        m = run_ref[0, :, cols]
        top = jnp.max(m, 0, keepdims=True)
        mf_ref[:, cols] = top
        tmp_ref[0, t:t + 1, :] = top
        tmp_ref[1, t:t + 1, :] = jnp.sum(run_ref[1, :, cols] * jnp.exp2(m - top), 0, keepdims=True)

    m_col = tmp_ref[0, 0:NT]
    gx_ref[me_x] = m_col + jnp.log2(tmp_ref[1, 0:NT])
    gX = exchange(lambda peer: gx_ref.at[me_x], gx_ref.at[me_x], me_x, NX, dev_x)

    def settle(first, last):
        def body(i, _):
            rows = ds(i * RC, RC)
            for t in range(T2 // CB):
                lanes = slice(t * CB, (t + 1) * CB)
                fix = jnp.exp2(cm_ref[i, :, lanes] - mf_ref[:, lanes])
                e = (p_ref[rows, lanes].reshape(RC // 8, 8, CB) * fix).reshape(RC, CB)
                p_ref[rows, lanes] = e
                hi = e.astype(BF16)
                hi_ref[rows, lanes] = hi
                lo_ref[rows, lanes] = (e - hi.astype(F32)).astype(BF16)
            return 0

        lax.fori_loop(first, last, body, 0)

    steps = S2 // RC
    settle(0, steps // 2)
    arrived(gX)
    gz_ref[me_z] = lse2(gx_ref, NX)
    gZ = exchange(lambda peer: gz_ref.at[me_z], gz_ref.at[me_z], me_z, NZ, dev_z)
    settle(steps // 2, steps)
    arrived(gZ)
    g_lse = lse2(gz_ref, NZ)
    k = jnp.exp2(m_col - g_lse)
    k_ref[...] = k
    b_mine = lb_ref[ds(me_c * NT, NT), :]
    w_ref[...] = k * jnp.exp(b_mine)

    def row_dots(i, _):
        rows = ds(i * RS, RS)
        acc = jnp.zeros((RS, L), F32)
        for t in range(NT):
            acc += p_ref[rows, t * L:(t + 1) * L] * w_ref[t:t + 1, :]
        sm_ref[rows, :] = acc
        return 0

    lax.fori_loop(0, S2 // RS, row_dots, 0)
    for i in range(NR):
        frc_ref[me_c, i:i + 1, :] = jnp.sum(sm_ref[i * L:(i + 1) * L, :].T, 0, keepdims=True)
    f2c = exchange(lambda peer: frc_ref.at[me_c], frc_ref.at[me_c], me_c, 2, dev_c)
    arrived(f2c)
    fr_ref[me_y] = add_up(frc_ref, 2)
    f2 = exchange(lambda peer: fr_ref.at[me_y], fr_ref.at[me_y], me_y, NY, dev_y)
    arrived(f2)
    total = add_up(fr_ref, NY)
    scale = jnp.exp(la) / total
    a_ref[...] = scale
    spread(scale)

    def column_dots(b, _):
        cols = ds(b * CB, CB)

        def step(i, acc):
            rows = ds(i * RS, RS)
            v = jnp.concatenate([vb_ref[rows, :]] * NX, 1)
            return acc + jnp.sum((p_ref[rows, cols] * v).reshape(RS // 8, 8, CB), 0)

        acc = lax.fori_loop(0, S2 // RS, step, jnp.zeros((8, CB), F32), unroll=2)
        acc = jnp.sum(acc, 0, keepdims=True)
        for t in range(NX):
            tmp_ref[0, pl.ds(b * NX + t, 1), :] = acc[:, t * L:(t + 1) * L]
        return 0

    lax.fori_loop(0, HZ, column_dots, 0)
    cx_ref[me_x] = tmp_ref[0, 0:NT] * k_ref[...]
    cX = exchange(lambda peer: cx_ref.at[me_x], cx_ref.at[me_x], me_x, NX, dev_x)

    mine = lambda v: jnp.where(me_c == 0, v[0:SR], v[SR:NR])
    potential = (jnp.log2(total) - la2 + lse) / BETA
    for i in range(SR):
        x = x_ref[:, i * L:(i + 1) * L]
        tmp_ref[1, i:i + 1, :] = jnp.sum(x * x, 0, keepdims=True) / E
    f_out[...] = tmp_ref[1, 0:SR] - mine(potential)

    for h in range(2):
        for i in range(SR):
            n = h * SR + i
            parts = split3(xs_ref[h, :, i * L:(i + 1) * L] * scale[n:n + 1, :])
            for j, part in enumerate(parts):
                xa_ref[j * E:(j + 1) * E, n * L:(n + 1) * L] = part

    def pulled(first, last):
        def body(b, _):
            cols = ds(b * CB, CB)
            out = jnp.dot(xa_ref[...], hi_ref[:, cols], preferred_element_type=F32)
            low = jnp.dot(xa_ref[0:2 * E, :], lo_ref[:, cols], preferred_element_type=F32)
            out = out[0:E] + out[E:2 * E] + out[2 * E:3 * E] + low[0:E] + low[E:2 * E]
            for t in range(NX):
                u_ref[t, b] = out[:, t * L:(t + 1) * L] * k_ref[pl.ds(b * NX + t, 1), :]
            return 0

        lax.fori_loop(first, last, body, 0)

    pulled(0, HZ // 2)
    arrived(cX)
    cz_ref[me_z] = add_up(cx_ref, NX)
    cZ = exchange(lambda peer: cz_ref.at[me_z], cz_ref.at[me_z], me_z, NZ, dev_z)
    H2 = HZ // 2
    uX = exchange(lambda peer: u_ref.at[peer, 0:H2], r1_ref.at[me_x, 0:H2], me_x, NX, dev_x)
    pulled(H2, HZ)
    uX += exchange(lambda peer: u_ref.at[peer, H2:HZ], r1_ref.at[me_x, H2:HZ], me_x, NX, dev_x)
    arrived(cZ)
    d = add_up(cz_ref, NZ)
    d_ref[...] = d
    tmp_ref[0, 0:NT] = w_ref[...] / d

    def prep_b(b, _):
        cols = ds(b * CB, CB)
        right = jnp.concatenate([tmp_ref[0, pl.ds(b * NX + t, 1), :] for t in range(NX)], 1)
        for j, part in enumerate(split3(y_ref[:, cols] * right)):
            yb_ref[j * E:(j + 1) * E, cols] = part
        b1, b2, b3 = split3(right)
        row = lax.broadcasted_iota(jnp.int32, (E, CB), 0)
        pick = lambda n, v: jnp.where(row == n, jnp.broadcast_to(v.astype(F32), (E, CB)), 0.0)
        yb_ref[3 * E:4 * E, cols] = (pick(0, b1) + pick(1, b2) + pick(2, b3)).astype(BF16)
        return 0

    lax.fori_loop(0, HZ, prep_b, 0)

    gs_ref[me_c] = (LOG2E * b_mine - g_lse - jnp.log2(d)) / BETA
    gC = exchange(lambda peer: gs_ref.at[me_c], gs_ref.at[me_c], me_c, 2, dev_c)

    core_base = sends.reserve(2)
    tgt_base = sends.reserve(2 * NY)
    RH = RB // 2

    def core_copy(n):
        return sends.copy(so_ref.at[n], sc_ref.at[n], core_base + n, core_base + n, partner)

    def tgt_copy(n, owner, sender):
        base = tgt_base + n * NY
        return sends.copy(sy_ref.at[n, owner], sr_ref.at[n, sender], base + owner, base + sender, dev_y(owner))

    def moved(h, n):
        starts = [h * S + j * RB + n * RH for j in range(NY)]
        nt = (((1,), (1,)), ((), ()))
        block = lambda ref: jnp.concatenate([ref[ds(start, RH), :] for start in starts], 0)
        out = lax.dot_general(block(hi_ref), yb_ref[...], nt, preferred_element_type=F32)
        out = out + lax.dot_general(block(lo_ref), yb_ref[...], nt, preferred_element_type=F32)
        out = out.T
        mass = out[3 * E:3 * E + 1] + out[3 * E + 1:3 * E + 2] + out[3 * E + 2:3 * E + 3]
        out = out[0:E] + out[E:2 * E] + out[2 * E:3 * E]
        terms = []
        for j in range(NY):
            here = slice(j * RH, (j + 1) * RH)
            x = xs_ref[h, :, ds(j * RB + n * RH, RH)]
            first = h * SR + (j * RB + n * RH) // L
            a = jnp.concatenate([a_ref[pl.ds(first + t, 1), :] for t in range(RH // L)], 1)
            terms.append((x * mass[:, here] - out[:, here]) * a)
        return terms

    def moved_other(n, _):
        for j, term in enumerate(moved(other, n)):
            so_ref[n, j] = term
        core_copy(n).start()
        return 0

    def moved_own(n):
        terms = moved(me_c, n)
        core_copy(n).wait_recv()
        for j, term in enumerate(terms):
            term = term + sc_ref[n, j]

            @pl.when(j == me_y)
            def _():
                sr_ref[n, me_y] = term

            @pl.when(j != me_y)
            def _():
                sy_ref[n, j] = term
                tgt_copy(n, j, me_y).start()

    lax.fori_loop(0, 2, moved_other, 0)
    moved_own(0)

    arrived(uX)
    for j in range(HZ):
        total = u_ref[me_x, j]
        for r in range(1, NX):
            total = total + r1_ref[lax.rem(me_x + r, NX), j]
        t2_ref[j] = total
    z_base = sends.reserve(NZ)
    first_z = me_c * HZ
    holds = me_z // HZ == me_c

    def z_copy(j, sender):
        return sends.copy(t2_ref.at[j], r2_ref.at[sender], z_base + j, z_base + sender, dev_z(first_z + j))

    for j in range(HZ):
        @pl.when(first_z + j != me_z)
        def _():
            z_copy(j, me_z).start()

    moved_own(1)

    sY = []
    for n in range(2):
        for j in range(NY):
            @pl.when(j != me_y)
            def _():
                tgt_copy(n, me_y, j).wait_recv()

        sgb_ref[n, me_y] = add_up(sr_ref.at[n], NY)
        sY += exchange(lambda peer: sgb_ref.at[n, me_y], sgb_ref.at[n, me_y], me_y, NY, dev_y)

    tile_base = sends.reserve(1)
    tile_copy = sends.copy(tile_ref, tile_ref, tile_base, tile_base, partner)

    @pl.when(holds)
    def _():
        for j in range(NZ):
            @pl.when(j != me_z)
            def _():
                z_copy(0, j).wait_recv()

        total = t2_ref[me_z - first_z]
        for r in range(1, NZ):
            total = total + r2_ref[lax.rem(me_z + r, NZ)]
        here = (me_z - first_z) * NX + me_x
        b = jnp.exp(lb_ref[pl.ds(me_z * NX + me_x, 1), :])
        y = y_ref[:, ds(here * L, L)]
        tile_ref[...] = b * (y - total / d_ref[pl.ds(here, 1), :])
        tile_copy.start()

    @pl.when(jnp.logical_not(holds))
    def _():
        tile_copy.wait_recv()

    tile = tile_ref[...]
    tg_out[:, 0, :] = jnp.where(me_c == 0, tile[:, 0:E], tile[:, E:2 * E])

    arrived(gC)
    g_out[0:NT] = gs_ref[0]
    g_out[NT:2 * NT] = gs_ref[1]

    arrived(sY)
    for n in range(2):
        for j in range(NY):
            sg_out[:, j * RB + n * RH:j * RB + (n + 1) * RH] = sgb_ref[n, j]

    for copy in sends.live:
        copy.wait_send()
    for n in range(2):
        core_copy(n).wait_send()
        for j in range(NY):
            @pl.when(j != me_y)
            def _():
                tgt_copy(n, j, me_y).wait_send()

    for j in range(HZ):
        @pl.when(first_z + j != me_z)
        def _():
            z_copy(j, me_z).wait_send()

    @pl.when(holds)
    def _():
        tile_copy.wait_send()


def finish_kernel(*refs):
    n = len(refs) // 2
    copies = [pltpu.make_async_copy(refs[i], refs[n + i], refs[-1].at[i]) for i in range(n)]
    for copy in copies:
        copy.start()
    for copy in copies:
        copy.wait()


def finish(*arrays):
    return pl.pallas_call(
        finish_kernel,
        out_shape=tuple(jax.ShapeDtypeStruct(a.shape, a.dtype) for a in arrays),
        in_specs=[pl.BlockSpec(memory_space=pl.ANY)] * len(arrays),
        out_specs=[pl.BlockSpec(memory_space=pl.ANY)] * len(arrays),
        scratch_shapes=[pltpu.SemaphoreType.DMA((len(arrays),))],
        compiler_params=pltpu.CompilerParams(vmem_limit_bytes=58 * 1024 * 1024),
        name="results",
    )(*arrays)


def local(dims, x, y, la, lb):
    NX, NZ, NY = dims
    E, S = x.shape
    T = y.shape[1]
    S2, T2 = 2 * S, T // 2
    HZ, RB = NZ // 2, S // NY
    NT, NR, SR = T2 // L, S2 // L, S // L
    n_sems = 2 + 2 * NY + 4 * (NX - 1) + 2 * (NZ - 1) + 1 + 2 + 2 * NY + NZ + 2 * (NY - 1) + 1
    big = max(NT, NR)
    vmem = lambda shape, dtype=F32: pltpu.VMEM(shape, dtype)
    f, g, sg, tg = pl.pallas_call(
        functools.partial(kernel, dims),
        out_shape=(
            jax.ShapeDtypeStruct((SR, L), F32),
            jax.ShapeDtypeStruct((2 * NT, L), F32),
            jax.ShapeDtypeStruct((E, S), F32),
            jax.ShapeDtypeStruct((E, 1, 64), F32),
        ),
        in_specs=[pl.BlockSpec(memory_space=pl.ANY if i == 1 else pltpu.VMEM) for i in range(4)],
        out_specs=[pl.BlockSpec(memory_space=pltpu.VMEM)] * 4,
        scratch_shapes=[
            vmem((S2, T2)), vmem((S2, T2), BF16), vmem((S2, T2), BF16),
            vmem((S2, 8 * E), BF16), vmem((8 * E, T2), BF16),
            vmem((S2, L)), vmem((S2, L)), vmem((S2, L)),
            vmem((S2 // RC, 8, T2)), vmem((1, T2)),
            vmem((2, E, S)), vmem((2, SR, L)), vmem((2, big, L)),
            vmem((2, 8, T2)), vmem((2, NR, L)), vmem((NY, NR, L)), vmem((2, NR, L)), vmem((NY, NR, L)),
            vmem((NX, NT, L)), vmem((NX, NT, L)), vmem((NZ, NT, L)), vmem((NT, L)), vmem((NT, L)),
            vmem((NR, L)), vmem((3 * E, S2), BF16), vmem((4 * E, T2), BF16),
            vmem((NX, NT, L)), vmem((NZ, NT, L)), vmem((NT, L)), vmem((2, NT, L)),
            vmem((NX, HZ, E, L)), vmem((NX, HZ, E, L)), vmem((HZ, E, L)), vmem((NZ, E, L)), vmem((E, L)),
            vmem((2, NY, E, RB // 2)), vmem((2, NY, E, RB // 2)),
            vmem((2, NY, E, RB // 2)), vmem((2, NY, E, RB // 2)), vmem((2, NY, E, RB // 2)),
            vmem((E, T2)),
            pltpu.SemaphoreType.DMA((n_sems,)), pltpu.SemaphoreType.DMA((n_sems,)), pltpu.SemaphoreType.DMA((HZ,)),
        ],
        compiler_params=pltpu.CompilerParams(
            collective_id=0, has_side_effects=True, vmem_limit_bytes=58 * 1024 * 1024
        ),
        cost_estimate=pl.CostEstimate(
            flops=2 * S2 * T2 * (8 + 5 + 8) * E, bytes_accessed=8 * E * (S + T), transcendentals=2 * S2 * T2
        ),
        name="sinkhorn",
    )(x, y, la.reshape(SR, L), lb.reshape(2 * NT, L))
    f, g, sg, tg = finish(f, g, sg, tg)
    return f.reshape(S), g.reshape(T), sg, tg


def solution(mesh):
    n_src, n_tgt = mesh.shape["src"], mesh.shape["tgt"]
    n_x = int(round((n_src // 4) ** 0.5))
    dims = (n_x, n_src // (2 * n_x), n_tgt)
    placed = (P(None, "src"), P(None, "tgt"), P("src"), P("tgt"))
    return jax.shard_map(
        functools.partial(local, dims),
        mesh=mesh,
        in_specs=placed,
        out_specs=(P("src"), P("tgt"), P(None, "src"), P(None, "tgt", "src")),
        check_vma=False,
    )
```

```python
import functools

import jax
import jax.numpy as jnp
import numpy as np
from jax import lax
from jax.experimental import pallas as pl
from jax.experimental.pallas import tpu as pltpu
from jax.sharding import PartitionSpec as P

EPSILON = 0.05
LOG2E = float(np.log2(np.e))
BETA = LOG2E / EPSILON
MESH = pl.DeviceIdType.MESH
F32 = jnp.float32
BF16 = jnp.bfloat16
RS = 128
RC = 64
L = 128


def split3(a):
    hi = a.astype(BF16)
    rest = a - hi.astype(F32)
    mid = rest.astype(BF16)
    lo = (rest - mid.astype(F32)).astype(BF16)
    return hi, mid, lo


def ds(start, size):
    return pl.ds(pl.multiple_of(start, size), size)


def lse2(ref, n):
    top = ref[0]
    for j in range(1, n):
        top = jnp.maximum(top, ref[j])
    total = jnp.exp2(ref[0] - top)
    for j in range(1, n):
        total = total + jnp.exp2(ref[j] - top)
    return top + jnp.log2(total)


def add_up(ref, n):
    total = ref[0]
    for j in range(1, n):
        total = total + ref[j]
    return total


class Sends:
    def __init__(self, send_sems, recv_sems):
        self.send_sems, self.recv_sems = send_sems, recv_sems
        self.taken = 0
        self.live = []

    def reserve(self, n):
        self.taken += n
        return self.taken - n

    def copy(self, src, dst, send, recv, device):
        return pltpu.make_async_remote_copy(
            src_ref=src,
            dst_ref=dst,
            send_sem=self.send_sems.at[send],
            recv_sem=self.recv_sems.at[recv],
            device_id=device,
            device_id_type=MESH,
        )

    def exchange(self, src, dst, me, n, device):
        base = self.reserve(n - 1)
        copies = []
        for r in range(1, n):
            peer = lax.rem(me + r, n)
            copies.append(self.copy(src(peer), dst, base + r - 1, base + r - 1, device(peer)))
        for copy in copies:
            copy.start()
        self.live += copies
        return copies


def arrived(copies):
    for copy in copies:
        copy.wait_recv()


def kernel(dims, x_ref, y_hbm, la_ref, lb_ref,
           f_out, g_out, sg_out, tg_out,
           p_ref, hi_ref, lo_ref, xk_ref, yk_ref, mx_ref, sm_ref, vb_ref, cm_ref, mf_ref,
           xs_ref, las_ref, tmp_ref, run_ref, fc_ref, fm_ref, frc_ref, fr_ref, gm_ref, gx_ref, gz_ref, k_ref, w_ref,
           a_ref, xa_ref, yb_ref, cx_ref, cz_ref, d_ref, gs_ref,
           u_ref, r1_ref, t2_ref, r2_ref, tile_ref, so_ref, sc_ref, sy_ref, sr_ref, sgb_ref,
           y_ref, send_sems, recv_sems, y_sems):
    NX, NZ, NY = dims
    NQ = 2 * NX
    E, S = x_ref.shape
    T = y_hbm.shape[1]
    T2, S2 = T // 2, 2 * S
    HZ = NZ // 2
    CB = NX * L
    RB = S // NY
    NT, NR, SR = T2 // L, S2 // L, S // L

    src = lax.axis_index("src")
    me_y = lax.axis_index("tgt")
    me_z = src // NQ
    me_q = lax.rem(src, NQ)
    me_x = me_q // 2
    me_c = lax.rem(me_q, 2)
    other = 1 - me_c
    chip = src - me_c

    dev_c = lambda j: {"src": chip + j}
    dev_y = lambda j: {"tgt": j}
    dev_z = lambda j: {"src": j * NQ + me_q}
    dev_x = lambda j: {"src": me_z * NQ + j * 2 + me_c}
    partner = {"src": chip + other}

    sends = Sends(send_sems, recv_sems)
    exchange = sends.exchange

    loads = [
        pltpu.make_async_copy(
            y_hbm.at[:, ds(me_c * T2 + b * CB, CB)], y_ref.at[:, b * CB:(b + 1) * CB], y_sems.at[b]
        )
        for b in range(HZ)
    ]
    for load in loads:
        load.start()

    barrier = pltpu.get_barrier_semaphore()
    greeted = 0
    for me, n, device in ((me_c, 2, dev_c), (me_y, NY, dev_y), (me_x, NX, dev_x), (me_z, NZ, dev_z)):
        for r in range(1, n):
            pl.semaphore_signal(barrier, inc=1, device_id=device(lax.rem(me + r, n)), device_id_type=MESH)
            greeted += 1

    def prep_y(b, _):
        cols = ds(b * CB, CB)
        y = y_ref[:, cols]
        y1, y2, y3 = split3(y)
        for n, part in enumerate((y1, y2, y1, y3, y2, y1)):
            yk_ref[n * E:(n + 1) * E, cols] = part
        lb = jnp.concatenate([lb_ref[pl.ds(me_c * NT + b * NX + t, 1), :] for t in range(NX)], 1)
        u = LOG2E * lb - (BETA / E) * jnp.sum(y * y, 0, keepdims=True)
        u1, u2, u3 = split3(u)
        row = lax.broadcasted_iota(jnp.int32, (16, CB), 0)
        pick = lambda n, v: jnp.where(row == n, jnp.broadcast_to(v.astype(F32), (16, CB)), 0.0)
        yk_ref[6 * E:6 * E + 16, cols] = (pick(0, u1) + pick(1, u2) + pick(2, u3)).astype(BF16)
        yk_ref[6 * E + 16:8 * E, cols] = jnp.zeros((2 * E - 16, CB), BF16)
        return 0


    lane = lax.broadcasted_iota(jnp.int32, (L, L), 1)
    left = lane < E

    def prep_x(h):
        def body(i, _):
            rows = ds(h * S + i * L, L)
            x = xs_ref[h, :, ds(i * L, L)] * (2.0 * BETA / E)
            x1, x2, x3 = (v.astype(F32) for v in split3(jnp.concatenate([x, x], 0).T))
            xk_ref[rows, 0:128] = x1.astype(BF16)
            xk_ref[rows, 128:256] = jnp.where(left, x2, x1).astype(BF16)
            xk_ref[rows, 256:384] = jnp.where(left, x2, x3).astype(BF16)
            xk_ref[rows, 384:512] = jnp.where(lane < 3, 1.0, 0.0).astype(BF16)
            mx_ref[rows, :] = jnp.full((L, L), -3e38, F32)
            sm_ref[rows, :] = jnp.zeros((L, L), F32)
            return 0

        lax.fori_loop(0, SR, body, 0)

    W2 = T2 // 2

    def scores(h, b):
        yk = yk_ref[:, b * W2:(b + 1) * W2]
        for i in range(S // RS):
            rows = ds(h * S + i * RS, RS)
            s = jnp.dot(xk_ref[rows, :], yk, preferred_element_type=F32)
            p_ref[rows, b * W2:(b + 1) * W2] = s
            old = mx_ref[rows, :]
            m = old
            for t in range(W2 // L):
                m = jnp.maximum(m, s[:, t * L:(t + 1) * L])
            acc = sm_ref[rows, :] * jnp.exp2(old - m)
            for t in range(W2 // L):
                acc = acc + jnp.exp2(s[:, t * L:(t + 1) * L] - m)
            mx_ref[rows, :] = m
            sm_ref[rows, :] = acc

    xs_ref[me_c] = x_ref[...]
    las_ref[me_c] = la_ref[...]
    prep_x(me_c)
    for load in loads:
        load.wait()
    lax.fori_loop(0, HZ, prep_y, 0)
    scores(me_c, 0)
    pl.semaphore_wait(barrier, greeted)
    base = sends.reserve(2)
    swap = [
        sends.copy(x_ref, xs_ref.at[me_c], base, base, partner),
        sends.copy(la_ref, las_ref.at[me_c], base + 1, base + 1, partner),
    ]
    for copy in swap:
        copy.start()
    sends.live += swap
    scores(me_c, 1)
    arrived(swap)
    prep_x(other)
    scores(other, 0)
    scores(other, 1)

    for i in range(NR):
        rows = slice(i * L, (i + 1) * L)
        m = mx_ref[rows, :].T
        top = jnp.max(m, 0, keepdims=True)
        tmp_ref[0, i:i + 1, :] = top
        tmp_ref[1, i:i + 1, :] = jnp.sum(sm_ref[rows, :].T * jnp.exp2(m - top), 0, keepdims=True)
    fc_ref[me_c] = tmp_ref[0] + jnp.log2(tmp_ref[1])
    f1c = exchange(lambda peer: fc_ref.at[me_c], fc_ref.at[me_c], me_c, 2, dev_c)

    la = jnp.concatenate([las_ref[0], las_ref[1]], 0)
    la2 = LOG2E * la

    def spread(a):
        for i in range(NR):
            vb_ref[i * L:(i + 1) * L, :] = jnp.broadcast_to(a[i:i + 1, :], (L, L)).T

    arrived(f1c)
    fm_ref[me_y] = lse2(fc_ref, 2)
    f1 = exchange(lambda peer: fm_ref.at[me_y], fm_ref.at[me_y], me_y, NY, dev_y)
    run_ref[0] = jnp.full((8, T2), -3e38, F32)
    run_ref[1] = jnp.zeros((8, T2), F32)
    arrived(f1)
    lse = lse2(fm_ref, NY)
    spread(la2 - lse)

    def columns(i, _):
        rows = ds(i * RC, RC)
        v = jnp.concatenate([vb_ref[rows, :]] * NX, 1)
        for b in range(HZ):
            cols = slice(b * CB, (b + 1) * CB)
            t = (p_ref[rows, cols] + v).reshape(RC // 8, 8, CB)
            old = run_ref[0, :, cols]
            m = jnp.maximum(old, jnp.max(t, 0))
            e = jnp.exp2(t - m)
            p_ref[rows, cols] = e.reshape(RC, CB)
            cm_ref[i, :, cols] = m
            run_ref[0, :, cols] = m
            run_ref[1, :, cols] = run_ref[1, :, cols] * jnp.exp2(old - m) + jnp.sum(e, 0)
        return 0

    lax.fori_loop(0, S2 // RC, columns, 0)
    for t in range(NT):
        cols = slice(t * L, (t + 1) * L)
        m = run_ref[0, :, cols]
        top = jnp.max(m, 0, keepdims=True)
        mf_ref[:, cols] = top
        tmp_ref[0, t:t + 1, :] = top
        tmp_ref[1, t:t + 1, :] = jnp.sum(run_ref[1, :, cols] * jnp.exp2(m - top), 0, keepdims=True)

    m_col = tmp_ref[0, 0:NT]
    gx_ref[me_x] = m_col + jnp.log2(tmp_ref[1, 0:NT])
    gX = exchange(lambda peer: gx_ref.at[me_x], gx_ref.at[me_x], me_x, NX, dev_x)

    def settle(first, last):
        def body(i, _):
            rows = ds(i * RC, RC)
            for t in range(T2 // CB):
                lanes = slice(t * CB, (t + 1) * CB)
                fix = jnp.exp2(cm_ref[i, :, lanes] - mf_ref[:, lanes])
                e = (p_ref[rows, lanes].reshape(RC // 8, 8, CB) * fix).reshape(RC, CB)
                p_ref[rows, lanes] = e
                hi = e.astype(BF16)
                hi_ref[rows, lanes] = hi
                lo_ref[rows, lanes] = (e - hi.astype(F32)).astype(BF16)
            return 0

        lax.fori_loop(first, last, body, 0)

    steps = S2 // RC
    settle(0, steps // 2)
    arrived(gX)
    gz_ref[me_z] = lse2(gx_ref, NX)
    gZ = exchange(lambda peer: gz_ref.at[me_z], gz_ref.at[me_z], me_z, NZ, dev_z)
    settle(steps // 2, steps)
    arrived(gZ)
    g_lse = lse2(gz_ref, NZ)
    k = jnp.exp2(m_col - g_lse)
    k_ref[...] = k
    b_mine = lb_ref[ds(me_c * NT, NT), :]
    w_ref[...] = k * jnp.exp(b_mine)

    def row_dots(i, _):
        rows = ds(i * RS, RS)
        acc = jnp.zeros((RS, L), F32)
        for t in range(NT):
            acc += p_ref[rows, t * L:(t + 1) * L] * w_ref[t:t + 1, :]
        sm_ref[rows, :] = acc
        return 0

    lax.fori_loop(0, S2 // RS, row_dots, 0)
    for i in range(NR):
        frc_ref[me_c, i:i + 1, :] = jnp.sum(sm_ref[i * L:(i + 1) * L, :].T, 0, keepdims=True)
    f2c = exchange(lambda peer: frc_ref.at[me_c], frc_ref.at[me_c], me_c, 2, dev_c)
    arrived(f2c)
    fr_ref[me_y] = add_up(frc_ref, 2)
    f2 = exchange(lambda peer: fr_ref.at[me_y], fr_ref.at[me_y], me_y, NY, dev_y)
    arrived(f2)
    total = add_up(fr_ref, NY)
    scale = jnp.exp(la) / total
    a_ref[...] = scale
    spread(scale)

    def column_dots(b, _):
        cols = ds(b * CB, CB)

        def step(i, acc):
            rows = ds(i * RS, RS)
            v = jnp.concatenate([vb_ref[rows, :]] * NX, 1)
            return acc + jnp.sum((p_ref[rows, cols] * v).reshape(RS // 8, 8, CB), 0)

        acc = lax.fori_loop(0, S2 // RS, step, jnp.zeros((8, CB), F32), unroll=2)
        acc = jnp.sum(acc, 0, keepdims=True)
        for t in range(NX):
            tmp_ref[0, pl.ds(b * NX + t, 1), :] = acc[:, t * L:(t + 1) * L]
        return 0

    lax.fori_loop(0, HZ, column_dots, 0)
    cx_ref[me_x] = tmp_ref[0, 0:NT] * k_ref[...]
    cX = exchange(lambda peer: cx_ref.at[me_x], cx_ref.at[me_x], me_x, NX, dev_x)

    mine = lambda v: jnp.where(me_c == 0, v[0:SR], v[SR:NR])
    potential = (jnp.log2(total) - la2 + lse) / BETA
    for i in range(SR):
        x = x_ref[:, i * L:(i + 1) * L]
        tmp_ref[1, i:i + 1, :] = jnp.sum(x * x, 0, keepdims=True) / E
    f_out[...] = tmp_ref[1, 0:SR] - mine(potential)

    for h in range(2):
        for i in range(SR):
            n = h * SR + i
            parts = split3(xs_ref[h, :, i * L:(i + 1) * L] * scale[n:n + 1, :])
            for j, part in enumerate(parts):
                xa_ref[j * E:(j + 1) * E, n * L:(n + 1) * L] = part

    def pulled(first, last):
        def body(b, _):
            cols = ds(b * CB, CB)
            out = jnp.dot(xa_ref[...], hi_ref[:, cols], preferred_element_type=F32)
            low = jnp.dot(xa_ref[0:2 * E, :], lo_ref[:, cols], preferred_element_type=F32)
            out = out[0:E] + out[E:2 * E] + out[2 * E:3 * E] + low[0:E] + low[E:2 * E]
            for t in range(NX):
                u_ref[t, b] = out[:, t * L:(t + 1) * L] * k_ref[pl.ds(b * NX + t, 1), :]
            return 0

        lax.fori_loop(first, last, body, 0)

    pulled(0, HZ // 2)
    arrived(cX)
    cz_ref[me_z] = add_up(cx_ref, NX)
    cZ = exchange(lambda peer: cz_ref.at[me_z], cz_ref.at[me_z], me_z, NZ, dev_z)
    H2 = HZ // 2
    uX = exchange(lambda peer: u_ref.at[peer, 0:H2], r1_ref.at[me_x, 0:H2], me_x, NX, dev_x)
    pulled(H2, HZ)
    uX += exchange(lambda peer: u_ref.at[peer, H2:HZ], r1_ref.at[me_x, H2:HZ], me_x, NX, dev_x)
    arrived(cZ)
    d = add_up(cz_ref, NZ)
    d_ref[...] = d
    tmp_ref[0, 0:NT] = w_ref[...] / d

    def prep_b(b, _):
        cols = ds(b * CB, CB)
        right = jnp.concatenate([tmp_ref[0, pl.ds(b * NX + t, 1), :] for t in range(NX)], 1)
        for j, part in enumerate(split3(y_ref[:, cols] * right)):
            yb_ref[j * E:(j + 1) * E, cols] = part
        b1, b2, b3 = split3(right)
        row = lax.broadcasted_iota(jnp.int32, (E, CB), 0)
        pick = lambda n, v: jnp.where(row == n, jnp.broadcast_to(v.astype(F32), (E, CB)), 0.0)
        yb_ref[3 * E:4 * E, cols] = (pick(0, b1) + pick(1, b2) + pick(2, b3)).astype(BF16)
        return 0

    lax.fori_loop(0, HZ, prep_b, 0)

    gs_ref[me_c] = (LOG2E * b_mine - g_lse - jnp.log2(d)) / BETA
    gC = exchange(lambda peer: gs_ref.at[me_c], gs_ref.at[me_c], me_c, 2, dev_c)

    core_base = sends.reserve(2)
    tgt_base = sends.reserve(2 * NY)
    RH = RB // 2

    def core_copy(n):
        return sends.copy(so_ref.at[n], sc_ref.at[n], core_base + n, core_base + n, partner)

    def tgt_copy(n, r):
        sem = tgt_base + n * NY + r
        return sends.copy(sy_ref.at[n, r], sr_ref.at[n, me_y], sem, sem, dev_y(lax.rem(me_y + r, NY)))

    owners = [lax.rem(me_y + r, NY) for r in range(NY)]

    def dots(h, n):
        nt = (((1,), (1,)), ((), ()))
        block = lambda ref: jnp.concatenate([ref[ds(h * S + j * RB + n * RH, RH), :] for j in owners], 0)
        out = lax.dot_general(block(hi_ref), yb_ref[...], nt, preferred_element_type=F32)
        return out + lax.dot_general(block(lo_ref), yb_ref[...], nt, preferred_element_type=F32)

    def terms(h, n, out):
        out = out.T
        mass = out[3 * E:3 * E + 1] + out[3 * E + 1:3 * E + 2] + out[3 * E + 2:3 * E + 3]
        out = out[0:E] + out[E:2 * E] + out[2 * E:3 * E]
        result = []
        for r, j in enumerate(owners):
            here = slice(r * RH, (r + 1) * RH)
            x = xs_ref[h, :, ds(j * RB + n * RH, RH)]
            first = h * SR + (j * RB + n * RH) // L
            a = jnp.concatenate([a_ref[pl.ds(first + t, 1), :] for t in range(RH // L)], 1)
            result.append((x * mass[:, here] - out[:, here]) * a)
        return result

    def to_partner(n, out):
        for r, term in enumerate(terms(other, n, out)):
            so_ref[n, owners[r]] = term
        core_copy(n).start()

    def to_owners(n, out):
        core_copy(n).wait_recv()
        for r, term in enumerate(terms(me_c, n, out)):
            term = term + sc_ref[n, owners[r]]
            if r == 0:
                sr_ref[n, me_y] = term
            else:
                sy_ref[n, r] = term
        for r in range(1, NY):
            tgt_copy(n, r).start()

    out0 = dots(other, 0)
    out1 = dots(other, 1)
    to_partner(0, out0)
    out2 = dots(me_c, 0)
    to_partner(1, out1)

    arrived(uX)
    for j in range(HZ):
        total = u_ref[me_x, j]
        for r in range(1, NX):
            total = total + r1_ref[lax.rem(me_x + r, NX), j]
        t2_ref[j] = total
    z_base = sends.reserve(NZ)
    first_z = me_c * HZ
    holds = me_z // HZ == me_c

    def z_copy(j, sender):
        return sends.copy(t2_ref.at[j], r2_ref.at[sender], z_base + j, z_base + sender, dev_z(first_z + j))

    for j in range(HZ):
        @pl.when(first_z + j != me_z)
        def _():
            z_copy(j, me_z).start()

    out3 = dots(me_c, 1)
    to_owners(0, out2)
    to_owners(1, out3)

    sY = []
    for n in range(2):
        for r in range(1, NY):
            tgt_copy(n, r).wait_recv()
        sgb_ref[n, me_y] = add_up(sr_ref.at[n], NY)
        sY += exchange(lambda peer: sgb_ref.at[n, me_y], sgb_ref.at[n, me_y], me_y, NY, dev_y)

    tile_base = sends.reserve(1)
    tile_copy = sends.copy(tile_ref, tile_ref, tile_base, tile_base, partner)

    @pl.when(holds)
    def _():
        for j in range(NZ):
            @pl.when(j != me_z)
            def _():
                z_copy(0, j).wait_recv()

        total = t2_ref[me_z - first_z]
        for r in range(1, NZ):
            total = total + r2_ref[lax.rem(me_z + r, NZ)]
        here = (me_z - first_z) * NX + me_x
        b = jnp.exp(lb_ref[pl.ds(me_z * NX + me_x, 1), :])
        y = y_ref[:, ds(here * L, L)]
        tile_ref[...] = b * (y - total / d_ref[pl.ds(here, 1), :])
        tile_copy.start()

    @pl.when(jnp.logical_not(holds))
    def _():
        tile_copy.wait_recv()

    tile = tile_ref[...]
    tg_out[:, 0, :] = jnp.where(me_c == 0, tile[:, 0:E], tile[:, E:2 * E])

    arrived(gC)
    g_out[0:NT] = gs_ref[0]
    g_out[NT:2 * NT] = gs_ref[1]

    arrived(sY)
    for n in range(2):
        for j in range(NY):
            sg_out[:, j * RB + n * RH:j * RB + (n + 1) * RH] = sgb_ref[n, j]

    for copy in sends.live:
        copy.wait_send()
    for n in range(2):
        core_copy(n).wait_send()
        for r in range(1, NY):
            tgt_copy(n, r).wait_send()
    for j in range(HZ):
        @pl.when(first_z + j != me_z)
        def _():
            z_copy(j, me_z).wait_send()

    @pl.when(holds)
    def _():
        tile_copy.wait_send()


def finish_kernel(*refs):
    n = len(refs) // 2
    for i in range(n):
        refs[n + i][...] = refs[i][...]


def finish(*arrays):
    return pl.pallas_call(
        finish_kernel,
        out_shape=tuple(jax.ShapeDtypeStruct(a.shape, a.dtype) for a in arrays),
        in_specs=[pl.BlockSpec(memory_space=pltpu.VMEM)] * len(arrays),
        out_specs=[pl.BlockSpec(memory_space=pltpu.VMEM)] * len(arrays),
        compiler_params=pltpu.CompilerParams(vmem_limit_bytes=58 * 1024 * 1024),
        name="results",
    )(*arrays)


def local(dims, x, y, la, lb):
    NX, NZ, NY = dims
    E, S = x.shape
    T = y.shape[1]
    S2, T2 = 2 * S, T // 2
    HZ, RB = NZ // 2, S // NY
    NT, NR, SR = T2 // L, S2 // L, S // L
    n_sems = 2 + 2 * NY + 4 * (NX - 1) + 2 * (NZ - 1) + 1 + 2 + 2 * NY + NZ + 2 * (NY - 1) + 1
    big = max(NT, NR)
    vmem = lambda shape, dtype=F32: pltpu.VMEM(shape, dtype)
    f, g, sg, tg = pl.pallas_call(
        functools.partial(kernel, dims),
        out_shape=(
            jax.ShapeDtypeStruct((SR, L), F32),
            jax.ShapeDtypeStruct((2 * NT, L), F32),
            jax.ShapeDtypeStruct((E, S), F32),
            jax.ShapeDtypeStruct((E, 1, 64), F32),
        ),
        in_specs=[pl.BlockSpec(memory_space=pl.ANY if i == 1 else pltpu.VMEM) for i in range(4)],
        out_specs=[pl.BlockSpec(memory_space=pltpu.VMEM)] * 4,
        scratch_shapes=[
            vmem((S2, T2)), vmem((S2, T2), BF16), vmem((S2, T2), BF16),
            vmem((S2, 8 * E), BF16), vmem((8 * E, T2), BF16),
            vmem((S2, L)), vmem((S2, L)), vmem((S2, L)),
            vmem((S2 // RC, 8, T2)), vmem((1, T2)),
            vmem((2, E, S)), vmem((2, SR, L)), vmem((2, big, L)),
            vmem((2, 8, T2)), vmem((2, NR, L)), vmem((NY, NR, L)), vmem((2, NR, L)), vmem((NY, NR, L)),
            vmem((NX, NT, L)), vmem((NX, NT, L)), vmem((NZ, NT, L)), vmem((NT, L)), vmem((NT, L)),
            vmem((NR, L)), vmem((3 * E, S2), BF16), vmem((4 * E, T2), BF16),
            vmem((NX, NT, L)), vmem((NZ, NT, L)), vmem((NT, L)), vmem((2, NT, L)),
            vmem((NX, HZ, E, L)), vmem((NX, HZ, E, L)), vmem((HZ, E, L)), vmem((NZ, E, L)), vmem((E, L)),
            vmem((2, NY, E, RB // 2)), vmem((2, NY, E, RB // 2)),
            vmem((2, NY, E, RB // 2)), vmem((2, NY, E, RB // 2)), vmem((2, NY, E, RB // 2)),
            vmem((E, T2)),
            pltpu.SemaphoreType.DMA((n_sems,)), pltpu.SemaphoreType.DMA((n_sems,)), pltpu.SemaphoreType.DMA((HZ,)),
        ],
        compiler_params=pltpu.CompilerParams(
            collective_id=0, has_side_effects=True, vmem_limit_bytes=58 * 1024 * 1024
        ),
        cost_estimate=pl.CostEstimate(
            flops=2 * S2 * T2 * (8 + 5 + 8) * E, bytes_accessed=8 * E * (S + T), transcendentals=2 * S2 * T2
        ),
        name="sinkhorn",
    )(x, y, la.reshape(SR, L), lb.reshape(2 * NT, L))
    f, g, sg, tg = finish(f, g, sg, tg)
    return f.reshape(S), g.reshape(T), sg, tg


def solution(mesh):
    n_src, n_tgt = mesh.shape["src"], mesh.shape["tgt"]
    n_x = int(round((n_src // 4) ** 0.5))
    dims = (n_x, n_src // (2 * n_x), n_tgt)
    placed = (P(None, "src"), P(None, "tgt"), P("src"), P("tgt"))
    return jax.shard_map(
        functools.partial(local, dims),
        mesh=mesh,
        in_specs=placed,
        out_specs=(P("src"), P("tgt"), P(None, "src"), P(None, "tgt", "src")),
        check_vma=False,
    )
```

```python
import functools

import jax
import jax.numpy as jnp
import numpy as np
from jax import lax
from jax.experimental import pallas as pl
from jax.experimental.pallas import tpu as pltpu
from jax.sharding import PartitionSpec as P

EPSILON = 0.05
LOG2E = float(np.log2(np.e))
BETA = LOG2E / EPSILON
MESH = pl.DeviceIdType.MESH
F32 = jnp.float32
BF16 = jnp.bfloat16
RS = 128
RC = 64
L = 128


def split3(a):
    hi = a.astype(BF16)
    rest = a - hi.astype(F32)
    mid = rest.astype(BF16)
    lo = (rest - mid.astype(F32)).astype(BF16)
    return hi, mid, lo


def ds(start, size):
    return pl.ds(pl.multiple_of(start, size), size)


def lse2(ref, n):
    top = ref[0]
    for j in range(1, n):
        top = jnp.maximum(top, ref[j])
    total = jnp.exp2(ref[0] - top)
    for j in range(1, n):
        total = total + jnp.exp2(ref[j] - top)
    return top + jnp.log2(total)


def add_up(ref, n):
    total = ref[0]
    for j in range(1, n):
        total = total + ref[j]
    return total


class Sends:
    def __init__(self, send_sems, recv_sems):
        self.send_sems, self.recv_sems = send_sems, recv_sems
        self.taken = 0
        self.live = []

    def reserve(self, n):
        self.taken += n
        return self.taken - n

    def copy(self, src, dst, send, recv, device):
        return pltpu.make_async_remote_copy(
            src_ref=src,
            dst_ref=dst,
            send_sem=self.send_sems.at[send],
            recv_sem=self.recv_sems.at[recv],
            device_id=device,
            device_id_type=MESH,
        )

    def exchange(self, src, dst, me, n, device):
        base = self.reserve(n - 1)
        copies = []
        for r in range(1, n):
            peer = lax.rem(me + r, n)
            copies.append(self.copy(src(peer), dst, base + r - 1, base + r - 1, device(peer)))
        for copy in copies:
            copy.start()
        self.live += copies
        return copies


def arrived(copies):
    for copy in copies:
        copy.wait_recv()


def kernel(dims, x_hbm, y_hbm, la_ref, lb_ref,
           f_out, g_out, sg_out, tg_out,
           p_ref, hi_ref, lo_ref, xk_ref, yk_ref, mx_ref, sm_ref, vb_ref, cm_ref, mf_ref,
           xs_ref, las_ref, tmp_ref, run_ref, fc_ref, fm_ref, frc_ref, fr_ref, gm_ref, gx_ref, gz_ref, k_ref, w_ref,
           a_ref, xa_ref, yb_ref, cx_ref, cz_ref, d_ref, gs_ref,
           u_ref, r1_ref, t2_ref, r2_ref, tile_ref, so_ref, sc_ref, sy_ref, sr_ref, sgb_ref,
           y_ref, f_ref, tg_ref, send_sems, recv_sems, y_sems, out_sems):
    NX, NZ, NY = dims
    NQ = 2 * NX
    E, S = x_hbm.shape
    T = y_hbm.shape[1]
    T2, S2 = T // 2, 2 * S
    HZ = NZ // 2
    CB = NX * L
    RB = S // NY
    NT, NR, SR = T2 // L, S2 // L, S // L

    src = lax.axis_index("src")
    me_y = lax.axis_index("tgt")
    me_z = src // NQ
    me_q = lax.rem(src, NQ)
    me_x = me_q // 2
    me_c = lax.rem(me_q, 2)
    other = 1 - me_c
    chip = src - me_c

    dev_c = lambda j: {"src": chip + j}
    dev_y = lambda j: {"tgt": j}
    dev_z = lambda j: {"src": j * NQ + me_q}
    dev_x = lambda j: {"src": me_z * NQ + j * 2 + me_c}
    partner = {"src": chip + other}

    sends = Sends(send_sems, recv_sems)
    exchange = sends.exchange

    loads = [
        pltpu.make_async_copy(
            y_hbm.at[:, ds(me_c * T2 + b * CB, CB)], y_ref.at[:, b * CB:(b + 1) * CB], y_sems.at[b]
        )
        for b in range(HZ)
    ]
    load_x = pltpu.make_async_copy(x_hbm, xs_ref.at[me_c], y_sems.at[HZ])
    load_x.start()
    for load in loads:
        load.start()

    writes = []

    def write(src_ref, out_ref):
        copy = pltpu.make_async_copy(src_ref, out_ref, out_sems.at[len(writes)])
        copy.start()
        writes.append(copy)

    barrier = pltpu.get_barrier_semaphore()
    greeted = 0
    for me, n, device in ((me_c, 2, dev_c), (me_y, NY, dev_y), (me_x, NX, dev_x), (me_z, NZ, dev_z)):
        for r in range(1, n):
            pl.semaphore_signal(barrier, inc=1, device_id=device(lax.rem(me + r, n)), device_id_type=MESH)
            greeted += 1

    def prep_y(b, _):
        cols = ds(b * CB, CB)
        y = y_ref[:, cols]
        y1, y2, y3 = split3(y)
        for n, part in enumerate((y1, y2, y1, y3, y2, y1)):
            yk_ref[n * E:(n + 1) * E, cols] = part
        lb = jnp.concatenate([lb_ref[pl.ds(me_c * NT + b * NX + t, 1), :] for t in range(NX)], 1)
        u = LOG2E * lb - (BETA / E) * jnp.sum(y * y, 0, keepdims=True)
        u1, u2, u3 = split3(u)
        row = lax.broadcasted_iota(jnp.int32, (16, CB), 0)
        pick = lambda n, v: jnp.where(row == n, jnp.broadcast_to(v.astype(F32), (16, CB)), 0.0)
        yk_ref[6 * E:6 * E + 16, cols] = (pick(0, u1) + pick(1, u2) + pick(2, u3)).astype(BF16)
        yk_ref[6 * E + 16:8 * E, cols] = jnp.zeros((2 * E - 16, CB), BF16)
        return 0


    lane = lax.broadcasted_iota(jnp.int32, (L, L), 1)
    left = lane < E

    def prep_x(h):
        def body(i, _):
            rows = ds(h * S + i * L, L)
            x = xs_ref[h, :, ds(i * L, L)] * (2.0 * BETA / E)
            x1, x2, x3 = (v.astype(F32) for v in split3(jnp.concatenate([x, x], 0).T))
            xk_ref[rows, 0:128] = x1.astype(BF16)
            xk_ref[rows, 128:256] = jnp.where(left, x2, x1).astype(BF16)
            xk_ref[rows, 256:384] = jnp.where(left, x2, x3).astype(BF16)
            xk_ref[rows, 384:512] = jnp.where(lane < 3, 1.0, 0.0).astype(BF16)
            mx_ref[rows, :] = jnp.full((L, L), -3e38, F32)
            sm_ref[rows, :] = jnp.zeros((L, L), F32)
            return 0

        lax.fori_loop(0, SR, body, 0)

    W2 = T2 // 2

    def scores(h, b):
        yk = yk_ref[:, b * W2:(b + 1) * W2]
        for i in range(S // RS):
            rows = ds(h * S + i * RS, RS)
            s = jnp.dot(xk_ref[rows, :], yk, preferred_element_type=F32)
            p_ref[rows, b * W2:(b + 1) * W2] = s
            old = mx_ref[rows, :]
            m = old
            for t in range(W2 // L):
                m = jnp.maximum(m, s[:, t * L:(t + 1) * L])
            acc = sm_ref[rows, :] * jnp.exp2(old - m)
            for t in range(W2 // L):
                acc = acc + jnp.exp2(s[:, t * L:(t + 1) * L] - m)
            mx_ref[rows, :] = m
            sm_ref[rows, :] = acc

    def merge(h):
        for i in range(SR):
            rows = ds(h * S + i * L, L)
            m = mx_ref[rows, :].T
            top = jnp.max(m, 0, keepdims=True)
            tmp_ref[0, pl.ds(h * SR + i, 1), :] = top
            tmp_ref[1, pl.ds(h * SR + i, 1), :] = jnp.sum(sm_ref[rows, :].T * jnp.exp2(m - top), 0, keepdims=True)

    load_x.wait()
    las_ref[me_c] = la_ref[...]
    prep_x(me_c)
    for load in loads:
        load.wait()
    lax.fori_loop(0, HZ, prep_y, 0)
    scores(me_c, 0)
    pl.semaphore_wait(barrier, greeted)
    base = sends.reserve(2)
    swap = [
        sends.copy(xs_ref.at[me_c], xs_ref.at[me_c], base, base, partner),
        sends.copy(la_ref, las_ref.at[me_c], base + 1, base + 1, partner),
    ]
    for copy in swap:
        copy.start()
    sends.live += swap
    scores(me_c, 1)
    arrived(swap)
    prep_x(other)
    merge(me_c)
    scores(other, 0)
    scores(other, 1)

    merge(other)
    fc_ref[me_c] = tmp_ref[0] + jnp.log2(tmp_ref[1])
    f1c = exchange(lambda peer: fc_ref.at[me_c], fc_ref.at[me_c], me_c, 2, dev_c)

    la = jnp.concatenate([las_ref[0], las_ref[1]], 0)
    la2 = LOG2E * la

    def spread(a):
        for i in range(NR):
            vb_ref[i * L:(i + 1) * L, :] = jnp.broadcast_to(a[i:i + 1, :], (L, L)).T

    arrived(f1c)
    fm_ref[me_y] = lse2(fc_ref, 2)
    f1 = exchange(lambda peer: fm_ref.at[me_y], fm_ref.at[me_y], me_y, NY, dev_y)
    run_ref[0] = jnp.full((8, T2), -3e38, F32)
    run_ref[1] = jnp.zeros((8, T2), F32)
    arrived(f1)
    lse = lse2(fm_ref, NY)
    spread(la2 - lse)

    def columns(i, _):
        rows = ds(i * RC, RC)
        v = jnp.concatenate([vb_ref[rows, :]] * NX, 1)
        for b in range(HZ):
            cols = slice(b * CB, (b + 1) * CB)
            t = (p_ref[rows, cols] + v).reshape(RC // 8, 8, CB)
            old = run_ref[0, :, cols]
            m = jnp.maximum(old, jnp.max(t, 0))
            e = jnp.exp2(t - m)
            p_ref[rows, cols] = e.reshape(RC, CB)
            cm_ref[i, :, cols] = m
            run_ref[0, :, cols] = m
            run_ref[1, :, cols] = run_ref[1, :, cols] * jnp.exp2(old - m) + jnp.sum(e, 0)
        return 0

    lax.fori_loop(0, S2 // RC, columns, 0)
    for t in range(NT):
        cols = slice(t * L, (t + 1) * L)
        m = run_ref[0, :, cols]
        top = jnp.max(m, 0, keepdims=True)
        mf_ref[:, cols] = top
        tmp_ref[0, t:t + 1, :] = top
        tmp_ref[1, t:t + 1, :] = jnp.sum(run_ref[1, :, cols] * jnp.exp2(m - top), 0, keepdims=True)

    m_col = tmp_ref[0, 0:NT]
    gx_ref[me_x] = m_col + jnp.log2(tmp_ref[1, 0:NT])
    gX = exchange(lambda peer: gx_ref.at[me_x], gx_ref.at[me_x], me_x, NX, dev_x)

    def settle(first, last):
        def body(i, _):
            rows = ds(i * RC, RC)
            for t in range(T2 // CB):
                lanes = slice(t * CB, (t + 1) * CB)
                fix = jnp.exp2(cm_ref[i, :, lanes] - mf_ref[:, lanes])
                e = (p_ref[rows, lanes].reshape(RC // 8, 8, CB) * fix).reshape(RC, CB)
                p_ref[rows, lanes] = e
                hi = e.astype(BF16)
                hi_ref[rows, lanes] = hi
                lo_ref[rows, lanes] = (e - hi.astype(F32)).astype(BF16)
            return 0

        lax.fori_loop(first, last, body, 0)

    steps = S2 // RC
    settle(0, steps // 2)
    arrived(gX)
    gz_ref[me_z] = lse2(gx_ref, NX)
    gZ = exchange(lambda peer: gz_ref.at[me_z], gz_ref.at[me_z], me_z, NZ, dev_z)
    settle(steps // 2, steps)
    arrived(gZ)
    g_lse = lse2(gz_ref, NZ)
    k = jnp.exp2(m_col - g_lse)
    k_ref[...] = k
    b_mine = lb_ref[ds(me_c * NT, NT), :]
    w_ref[...] = k * jnp.exp(b_mine)

    def row_dots(i, _):
        rows = ds(i * RS, RS)
        acc = jnp.zeros((RS, L), F32)
        for t in range(NT):
            acc += p_ref[rows, t * L:(t + 1) * L] * w_ref[t:t + 1, :]
        sm_ref[rows, :] = acc
        return 0

    lax.fori_loop(0, S2 // RS, row_dots, 0)
    for i in range(NR):
        frc_ref[me_c, i:i + 1, :] = jnp.sum(sm_ref[i * L:(i + 1) * L, :].T, 0, keepdims=True)
    f2c = exchange(lambda peer: frc_ref.at[me_c], frc_ref.at[me_c], me_c, 2, dev_c)
    arrived(f2c)
    fr_ref[me_y] = add_up(frc_ref, 2)
    f2 = exchange(lambda peer: fr_ref.at[me_y], fr_ref.at[me_y], me_y, NY, dev_y)
    arrived(f2)
    total = add_up(fr_ref, NY)
    scale = jnp.exp(la) / total
    a_ref[...] = scale
    spread(scale)

    def column_dots(b, _):
        cols = ds(b * CB, CB)

        def step(i, acc):
            rows = ds(i * RS, RS)
            v = jnp.concatenate([vb_ref[rows, :]] * NX, 1)
            return acc + jnp.sum((p_ref[rows, cols] * v).reshape(RS // 8, 8, CB), 0)

        acc = lax.fori_loop(0, S2 // RS, step, jnp.zeros((8, CB), F32), unroll=2)
        acc = jnp.sum(acc, 0, keepdims=True)
        for t in range(NX):
            tmp_ref[0, pl.ds(b * NX + t, 1), :] = acc[:, t * L:(t + 1) * L]
        return 0

    lax.fori_loop(0, HZ, column_dots, 0)
    cx_ref[me_x] = tmp_ref[0, 0:NT] * k_ref[...]
    cX = exchange(lambda peer: cx_ref.at[me_x], cx_ref.at[me_x], me_x, NX, dev_x)

    mine = lambda v: jnp.where(me_c == 0, v[0:SR], v[SR:NR])
    potential = (jnp.log2(total) - la2 + lse) / BETA
    for i in range(SR):
        x = xs_ref[me_c, :, i * L:(i + 1) * L]
        tmp_ref[1, i:i + 1, :] = jnp.sum(x * x, 0, keepdims=True) / E
    f_ref[...] = tmp_ref[1, 0:SR] - mine(potential)
    write(f_ref, f_out)

    for h in range(2):
        for i in range(SR):
            n = h * SR + i
            parts = split3(xs_ref[h, :, i * L:(i + 1) * L] * scale[n:n + 1, :])
            for j, part in enumerate(parts):
                xa_ref[j * E:(j + 1) * E, n * L:(n + 1) * L] = part

    def pulled(first, last):
        def body(b, _):
            cols = ds(b * CB, CB)
            out = jnp.dot(xa_ref[...], hi_ref[:, cols], preferred_element_type=F32)
            low = jnp.dot(xa_ref[0:2 * E, :], lo_ref[:, cols], preferred_element_type=F32)
            out = out[0:E] + out[E:2 * E] + out[2 * E:3 * E] + low[0:E] + low[E:2 * E]
            for t in range(NX):
                u_ref[t, b] = out[:, t * L:(t + 1) * L] * k_ref[pl.ds(b * NX + t, 1), :]
            return 0

        lax.fori_loop(first, last, body, 0)

    pulled(0, HZ // 2)
    arrived(cX)
    cz_ref[me_z] = add_up(cx_ref, NX)
    cZ = exchange(lambda peer: cz_ref.at[me_z], cz_ref.at[me_z], me_z, NZ, dev_z)
    H2 = HZ // 2
    uX = exchange(lambda peer: u_ref.at[peer, 0:H2], r1_ref.at[me_x, 0:H2], me_x, NX, dev_x)
    pulled(H2, HZ)
    uX += exchange(lambda peer: u_ref.at[peer, H2:HZ], r1_ref.at[me_x, H2:HZ], me_x, NX, dev_x)
    arrived(cZ)
    d = add_up(cz_ref, NZ)
    d_ref[...] = d
    tmp_ref[0, 0:NT] = w_ref[...] / d

    def prep_b(b, _):
        cols = ds(b * CB, CB)
        right = jnp.concatenate([tmp_ref[0, pl.ds(b * NX + t, 1), :] for t in range(NX)], 1)
        for j, part in enumerate(split3(y_ref[:, cols] * right)):
            yb_ref[j * E:(j + 1) * E, cols] = part
        b1, b2, b3 = split3(right)
        row = lax.broadcasted_iota(jnp.int32, (E, CB), 0)
        pick = lambda n, v: jnp.where(row == n, jnp.broadcast_to(v.astype(F32), (E, CB)), 0.0)
        yb_ref[3 * E:4 * E, cols] = (pick(0, b1) + pick(1, b2) + pick(2, b3)).astype(BF16)
        return 0

    lax.fori_loop(0, HZ, prep_b, 0)

    gs_ref[me_c] = (LOG2E * b_mine - g_lse - jnp.log2(d)) / BETA
    gC = exchange(lambda peer: gs_ref.at[me_c], gs_ref.at[me_c], me_c, 2, dev_c)

    core_base = sends.reserve(2)
    tgt_base = sends.reserve(2 * NY)
    RH = RB // 2

    def core_copy(n):
        return sends.copy(so_ref.at[n], sc_ref.at[n], core_base + n, core_base + n, partner)

    def tgt_copy(n, r):
        sem = tgt_base + n * NY + r
        return sends.copy(sy_ref.at[n, r], sr_ref.at[n, me_y], sem, sem, dev_y(lax.rem(me_y + r, NY)))

    owners = [lax.rem(me_y + r, NY) for r in range(NY)]

    def dots(h, n):
        nt = (((1,), (1,)), ((), ()))
        block = lambda ref: jnp.concatenate([ref[ds(h * S + j * RB + n * RH, RH), :] for j in owners], 0)
        out = lax.dot_general(block(hi_ref), yb_ref[...], nt, preferred_element_type=F32)
        return out + lax.dot_general(block(lo_ref), yb_ref[...], nt, preferred_element_type=F32)

    def terms(h, n, out):
        out = out.T
        mass = out[3 * E:3 * E + 1] + out[3 * E + 1:3 * E + 2] + out[3 * E + 2:3 * E + 3]
        out = out[0:E] + out[E:2 * E] + out[2 * E:3 * E]
        result = []
        for r, j in enumerate(owners):
            here = slice(r * RH, (r + 1) * RH)
            x = xs_ref[h, :, ds(j * RB + n * RH, RH)]
            first = h * SR + (j * RB + n * RH) // L
            a = jnp.concatenate([a_ref[pl.ds(first + t, 1), :] for t in range(RH // L)], 1)
            result.append((x * mass[:, here] - out[:, here]) * a)
        return result

    def to_partner(n, out):
        for r, term in enumerate(terms(other, n, out)):
            so_ref[n, owners[r]] = term
        core_copy(n).start()

    def to_owners(n, out):
        core_copy(n).wait_recv()
        for r, term in enumerate(terms(me_c, n, out)):
            term = term + sc_ref[n, owners[r]]
            if r == 0:
                sr_ref[n, me_y] = term
            else:
                sy_ref[n, r] = term
        for r in range(1, NY):
            tgt_copy(n, r).start()

    out0 = dots(other, 0)
    out1 = dots(other, 1)
    to_partner(0, out0)
    to_partner(1, out1)
    out2 = dots(me_c, 0)
    to_owners(0, out2)

    arrived(uX)
    for j in range(HZ):
        total = u_ref[me_x, j]
        for r in range(1, NX):
            total = total + r1_ref[lax.rem(me_x + r, NX), j]
        t2_ref[j] = total
    z_base = sends.reserve(NZ)
    first_z = me_c * HZ
    holds = me_z // HZ == me_c

    def z_copy(j, sender):
        return sends.copy(t2_ref.at[j], r2_ref.at[sender], z_base + j, z_base + sender, dev_z(first_z + j))

    for j in range(HZ):
        @pl.when(first_z + j != me_z)
        def _():
            z_copy(j, me_z).start()

    out3 = dots(me_c, 1)
    to_owners(1, out3)

    sY = []
    for n in range(2):
        for r in range(1, NY):
            tgt_copy(n, r).wait_recv()
        sgb_ref[n, me_y] = add_up(sr_ref.at[n], NY)
        sY.append(exchange(lambda peer: sgb_ref.at[n, me_y], sgb_ref.at[n, me_y], me_y, NY, dev_y))
        write(sgb_ref.at[n, me_y], sg_out.at[:, ds(me_y * RB + n * RH, RH)])

    tile_base = sends.reserve(1)
    tile_copy = sends.copy(tile_ref, tile_ref, tile_base, tile_base, partner)

    @pl.when(holds)
    def _():
        for j in range(NZ):
            @pl.when(j != me_z)
            def _():
                z_copy(0, j).wait_recv()

        total = t2_ref[me_z - first_z]
        for r in range(1, NZ):
            total = total + r2_ref[lax.rem(me_z + r, NZ)]
        here = (me_z - first_z) * NX + me_x
        b = jnp.exp(lb_ref[pl.ds(me_z * NX + me_x, 1), :])
        y = y_ref[:, ds(here * L, L)]
        tile_ref[...] = b * (y - total / d_ref[pl.ds(here, 1), :])
        tile_copy.start()

    @pl.when(jnp.logical_not(holds))
    def _():
        tile_copy.wait_recv()

    tile = tile_ref[...]
    tg_ref[:, 0, :] = jnp.where(me_c == 0, tile[:, 0:E], tile[:, E:2 * E])
    write(tg_ref, tg_out)

    arrived(gC)
    for j in range(2):
        write(gs_ref.at[j], g_out.at[j * NT:(j + 1) * NT])

    for n in range(2):
        for r in range(1, NY):
            sY[n][r - 1].wait_recv()
            j = lax.rem(me_y + NY - r, NY)
            write(sgb_ref.at[n, j], sg_out.at[:, ds(j * RB + n * RH, RH)])

    for copy in writes:
        copy.wait()
    for copy in sends.live:
        copy.wait_send()
    for n in range(2):
        core_copy(n).wait_send()
        for r in range(1, NY):
            tgt_copy(n, r).wait_send()
    for j in range(HZ):
        @pl.when(first_z + j != me_z)
        def _():
            z_copy(j, me_z).wait_send()

    @pl.when(holds)
    def _():
        tile_copy.wait_send()


def finish_kernel(*refs):
    n = len(refs) // 2
    for i in range(n):
        refs[n + i][...] = refs[i][...]


def finish(*arrays):
    return pl.pallas_call(
        finish_kernel,
        out_shape=tuple(jax.ShapeDtypeStruct(a.shape, a.dtype) for a in arrays),
        in_specs=[pl.BlockSpec(memory_space=pltpu.VMEM)] * len(arrays),
        out_specs=[pl.BlockSpec(memory_space=pltpu.VMEM)] * len(arrays),
        compiler_params=pltpu.CompilerParams(vmem_limit_bytes=58 * 1024 * 1024),
        name="results",
    )(*arrays)


def local(dims, x, y, la, lb):
    NX, NZ, NY = dims
    E, S = x.shape
    T = y.shape[1]
    S2, T2 = 2 * S, T // 2
    HZ, RB = NZ // 2, S // NY
    NT, NR, SR = T2 // L, S2 // L, S // L
    n_sems = 2 + 2 * NY + 4 * (NX - 1) + 2 * (NZ - 1) + 1 + 2 + 2 * NY + NZ + 2 * (NY - 1) + 1
    big = max(NT, NR)
    vmem = lambda shape, dtype=F32: pltpu.VMEM(shape, dtype)
    f, g, sg, tg = pl.pallas_call(
        functools.partial(kernel, dims),
        out_shape=(
            jax.ShapeDtypeStruct((SR, L), F32),
            jax.ShapeDtypeStruct((2 * NT, L), F32),
            jax.ShapeDtypeStruct((E, S), F32),
            jax.ShapeDtypeStruct((E, 1, 64), F32),
        ),
        in_specs=[pl.BlockSpec(memory_space=pl.ANY if i < 2 else pltpu.VMEM) for i in range(4)],
        out_specs=[pl.BlockSpec(memory_space=pl.ANY)] * 4,
        scratch_shapes=[
            vmem((S2, T2)), vmem((S2, T2), BF16), vmem((S2, T2), BF16),
            vmem((S2, 8 * E), BF16), vmem((8 * E, T2), BF16),
            vmem((S2, L)), vmem((S2, L)), vmem((S2, L)),
            vmem((S2 // RC, 8, T2)), vmem((1, T2)),
            vmem((2, E, S)), vmem((2, SR, L)), vmem((2, big, L)),
            vmem((2, 8, T2)), vmem((2, NR, L)), vmem((NY, NR, L)), vmem((2, NR, L)), vmem((NY, NR, L)),
            vmem((NX, NT, L)), vmem((NX, NT, L)), vmem((NZ, NT, L)), vmem((NT, L)), vmem((NT, L)),
            vmem((NR, L)), vmem((3 * E, S2), BF16), vmem((4 * E, T2), BF16),
            vmem((NX, NT, L)), vmem((NZ, NT, L)), vmem((NT, L)), vmem((2, NT, L)),
            vmem((NX, HZ, E, L)), vmem((NX, HZ, E, L)), vmem((HZ, E, L)), vmem((NZ, E, L)), vmem((E, L)),
            vmem((2, NY, E, RB // 2)), vmem((2, NY, E, RB // 2)),
            vmem((2, NY, E, RB // 2)), vmem((2, NY, E, RB // 2)), vmem((2, NY, E, RB // 2)),
            vmem((E, T2)), vmem((SR, L)), vmem((E, 1, 64)),
            pltpu.SemaphoreType.DMA((n_sems,)), pltpu.SemaphoreType.DMA((n_sems,)), pltpu.SemaphoreType.DMA((HZ + 1,)),
            pltpu.SemaphoreType.DMA((4 + 2 * NY,)),
        ],
        compiler_params=pltpu.CompilerParams(
            collective_id=0, has_side_effects=True, vmem_limit_bytes=58 * 1024 * 1024
        ),
        cost_estimate=pl.CostEstimate(
            flops=2 * S2 * T2 * (8 + 5 + 8) * E, bytes_accessed=8 * E * (S + T), transcendentals=2 * S2 * T2
        ),
        name="sinkhorn",
    )(x, y, la.reshape(SR, L), lb.reshape(2 * NT, L))
    f, g, sg, tg = finish(f, g, sg, tg)
    return f.reshape(S), g.reshape(T), sg, tg


def solution(mesh):
    n_src, n_tgt = mesh.shape["src"], mesh.shape["tgt"]
    n_x = int(round((n_src // 4) ** 0.5))
    dims = (n_x, n_src // (2 * n_x), n_tgt)
    placed = (P(None, "src"), P(None, "tgt"), P("src"), P("tgt"))
    return jax.shard_map(
        functools.partial(local, dims),
        mesh=mesh,
        in_specs=placed,
        out_specs=(P("src"), P("tgt"), P(None, "src"), P(None, "tgt", "src")),
        check_vma=False,
    )
```

```python
import functools

import jax
import jax.numpy as jnp
import numpy as np
from jax import lax
from jax.experimental import pallas as pl
from jax.experimental.pallas import tpu as pltpu
from jax.sharding import PartitionSpec as P

EPSILON = 0.05
LOG2E = float(np.log2(np.e))
BETA = LOG2E / EPSILON
MESH = pl.DeviceIdType.MESH
F32 = jnp.float32
BF16 = jnp.bfloat16
RS = 128
RC = 64
L = 128


def split3(a):
    hi = a.astype(BF16)
    rest = a - hi.astype(F32)
    mid = rest.astype(BF16)
    lo = (rest - mid.astype(F32)).astype(BF16)
    return hi, mid, lo


def ds(start, size):
    return pl.ds(pl.multiple_of(start, size), size)


def lse2(ref, n):
    top = ref[0]
    for j in range(1, n):
        top = jnp.maximum(top, ref[j])
    total = jnp.exp2(ref[0] - top)
    for j in range(1, n):
        total = total + jnp.exp2(ref[j] - top)
    return top + jnp.log2(total)


def add_up(ref, n):
    total = ref[0]
    for j in range(1, n):
        total = total + ref[j]
    return total


def far_first(n):
    return sorted(range(1, n), key=lambda r: -min(r, n - r))


class Sends:
    def __init__(self, send_sems, recv_sems):
        self.send_sems, self.recv_sems = send_sems, recv_sems
        self.taken = 0
        self.live = []

    def reserve(self, n):
        self.taken += n
        return self.taken - n

    def copy(self, src, dst, send, recv, device):
        return pltpu.make_async_remote_copy(
            src_ref=src,
            dst_ref=dst,
            send_sem=self.send_sems.at[send],
            recv_sem=self.recv_sems.at[recv],
            device_id=device,
            device_id_type=MESH,
        )

    def exchange(self, src, dst, me, n, device):
        base = self.reserve(n - 1)
        copies = []
        for r in range(1, n):
            peer = lax.rem(me + r, n)
            copies.append(self.copy(src(peer), dst, base + r - 1, base + r - 1, device(peer)))
        for r in far_first(n):
            copies[r - 1].start()
        self.live += copies
        return copies


def arrived(copies):
    for copy in copies:
        copy.wait_recv()


def kernel(dims, x_hbm, y_hbm, la_ref, lb_ref,
           f_out, g_out, sg_out, tg_out,
           p_ref, hi_ref, lo_ref, xk_ref, yk_ref, mx_ref, sm_ref, vb_ref, cm_ref, mf_ref,
           xs_ref, las_ref, tmp_ref, run_ref, fc_ref, fm_ref, frc_ref, fr_ref, gm_ref, gx_ref, gz_ref, k_ref, w_ref,
           a_ref, xa_ref, yb_ref, cx_ref, cz_ref, d_ref, gs_ref,
           u_ref, r1_ref, t2_ref, r2_ref, tile_ref, so_ref, sc_ref, sy_ref, sr_ref, sgb_ref,
           y_ref, f_ref, tg_ref, send_sems, recv_sems, y_sems, out_sems):
    NX, NZ, NY = dims
    NQ = 2 * NX
    E, S = x_hbm.shape
    T = y_hbm.shape[1]
    T2, S2 = T // 2, 2 * S
    HZ = NZ // 2
    CB = NX * L
    RB = S // NY
    NT, NR, SR = T2 // L, S2 // L, S // L

    src = lax.axis_index("src")
    me_y = lax.axis_index("tgt")
    me_z = src // NQ
    me_q = lax.rem(src, NQ)
    me_x = me_q // 2
    me_c = lax.rem(me_q, 2)
    other = 1 - me_c
    chip = src - me_c

    dev_c = lambda j: {"src": chip + j}
    dev_y = lambda j: {"tgt": j}
    dev_z = lambda j: {"src": j * NQ + me_q}
    dev_x = lambda j: {"src": me_z * NQ + j * 2 + me_c}
    partner = {"src": chip + other}

    sends = Sends(send_sems, recv_sems)
    exchange = sends.exchange

    loads = [
        pltpu.make_async_copy(
            y_hbm.at[:, ds(me_c * T2 + b * CB, CB)], y_ref.at[:, b * CB:(b + 1) * CB], y_sems.at[b]
        )
        for b in range(HZ)
    ]
    writes = []

    def write(src_ref, out_ref):
        copy = pltpu.make_async_copy(src_ref, out_ref, out_sems.at[len(writes)])
        copy.start()
        writes.append(copy)

    barrier = pltpu.get_barrier_semaphore()
    greeted = 0
    for me, n, device in ((me_z, NZ, dev_z), (me_x, NX, dev_x), (me_y, NY, dev_y), (me_c, 2, dev_c)):
        for r in far_first(n):
            pl.semaphore_signal(barrier, inc=1, device_id=device(lax.rem(me + r, n)), device_id_type=MESH)
            greeted += 1

    load_x = pltpu.make_async_copy(x_hbm, xs_ref.at[me_c], y_sems.at[HZ])
    load_x.start()
    for load in loads:
        load.start()

    def prep_y(b, _):
        cols = ds(b * CB, CB)
        y = y_ref[:, cols]
        y1, y2, y3 = split3(y)
        for n, part in enumerate((y1, y2, y1, y3, y2, y1)):
            yk_ref[n * E:(n + 1) * E, cols] = part
        lb = jnp.concatenate([lb_ref[pl.ds(me_c * NT + b * NX + t, 1), :] for t in range(NX)], 1)
        u = LOG2E * lb - (BETA / E) * jnp.sum(y * y, 0, keepdims=True)
        u1, u2, u3 = split3(u)
        row = lax.broadcasted_iota(jnp.int32, (16, CB), 0)
        pick = lambda n, v: jnp.where(row == n, jnp.broadcast_to(v.astype(F32), (16, CB)), 0.0)
        yk_ref[6 * E:6 * E + 16, cols] = (pick(0, u1) + pick(1, u2) + pick(2, u3)).astype(BF16)
        yk_ref[6 * E + 16:8 * E, cols] = jnp.zeros((2 * E - 16, CB), BF16)
        return 0


    lane = lax.broadcasted_iota(jnp.int32, (L, L), 1)
    left = lane < E

    def prep_x(h):
        def body(i, _):
            rows = ds(h * S + i * L, L)
            x = xs_ref[h, :, ds(i * L, L)] * (2.0 * BETA / E)
            x1, x2, x3 = (v.astype(F32) for v in split3(jnp.concatenate([x, x], 0).T))
            xk_ref[rows, 0:128] = x1.astype(BF16)
            xk_ref[rows, 128:256] = jnp.where(left, x2, x1).astype(BF16)
            xk_ref[rows, 256:384] = jnp.where(left, x2, x3).astype(BF16)
            xk_ref[rows, 384:512] = jnp.where(lane < 3, 1.0, 0.0).astype(BF16)
            mx_ref[rows, :] = jnp.full((L, L), -3e38, F32)
            sm_ref[rows, :] = jnp.zeros((L, L), F32)
            return 0

        lax.fori_loop(0, SR, body, 0)

    W2 = T2 // 2

    def scores(h, b):
        yk = yk_ref[:, b * W2:(b + 1) * W2]
        for i in range(S // RS):
            rows = ds(h * S + i * RS, RS)
            s = jnp.dot(xk_ref[rows, :], yk, preferred_element_type=F32)
            p_ref[rows, b * W2:(b + 1) * W2] = s
            old = mx_ref[rows, :]
            m = old
            for t in range(W2 // L):
                m = jnp.maximum(m, s[:, t * L:(t + 1) * L])
            acc = sm_ref[rows, :] * jnp.exp2(old - m)
            for t in range(W2 // L):
                acc = acc + jnp.exp2(s[:, t * L:(t + 1) * L] - m)
            mx_ref[rows, :] = m
            sm_ref[rows, :] = acc

    def merge(h):
        for i in range(SR):
            rows = ds(h * S + i * L, L)
            m = mx_ref[rows, :].T
            top = jnp.max(m, 0, keepdims=True)
            tmp_ref[0, pl.ds(h * SR + i, 1), :] = top
            tmp_ref[1, pl.ds(h * SR + i, 1), :] = jnp.sum(sm_ref[rows, :].T * jnp.exp2(m - top), 0, keepdims=True)

    load_x.wait()
    las_ref[me_c] = la_ref[...]
    prep_x(me_c)
    for load in loads:
        load.wait()
    lax.fori_loop(0, HZ, prep_y, 0)
    scores(me_c, 0)
    pl.semaphore_wait(barrier, greeted)
    base = sends.reserve(2)
    swap = [
        sends.copy(xs_ref.at[me_c], xs_ref.at[me_c], base, base, partner),
        sends.copy(la_ref, las_ref.at[me_c], base + 1, base + 1, partner),
    ]
    for copy in swap:
        copy.start()
    sends.live += swap
    scores(me_c, 1)
    arrived(swap)
    prep_x(other)
    merge(me_c)
    scores(other, 0)
    scores(other, 1)

    merge(other)
    fc_ref[me_c] = tmp_ref[0] + jnp.log2(tmp_ref[1])
    f1c = exchange(lambda peer: fc_ref.at[me_c], fc_ref.at[me_c], me_c, 2, dev_c)

    la = jnp.concatenate([las_ref[0], las_ref[1]], 0)
    la2 = LOG2E * la

    def spread(a):
        for i in range(NR):
            vb_ref[i * L:(i + 1) * L, :] = jnp.broadcast_to(a[i:i + 1, :], (L, L)).T

    arrived(f1c)
    fm_ref[me_y] = lse2(fc_ref, 2)
    f1 = exchange(lambda peer: fm_ref.at[me_y], fm_ref.at[me_y], me_y, NY, dev_y)
    run_ref[0] = jnp.full((8, T2), -3e38, F32)
    run_ref[1] = jnp.zeros((8, T2), F32)
    arrived(f1)
    lse = lse2(fm_ref, NY)
    spread(la2 - lse)

    def columns(i, _):
        rows = ds(i * RC, RC)
        v = jnp.concatenate([vb_ref[rows, :]] * NX, 1)
        for b in range(HZ):
            cols = slice(b * CB, (b + 1) * CB)
            t = (p_ref[rows, cols] + v).reshape(RC // 8, 8, CB)
            old = run_ref[0, :, cols]
            m = jnp.maximum(old, jnp.max(t, 0))
            e = jnp.exp2(t - m)
            p_ref[rows, cols] = e.reshape(RC, CB)
            cm_ref[i, :, cols] = m
            run_ref[0, :, cols] = m
            run_ref[1, :, cols] = run_ref[1, :, cols] * jnp.exp2(old - m) + jnp.sum(e, 0)
        return 0

    lax.fori_loop(0, S2 // RC, columns, 0)
    for t in range(NT):
        cols = slice(t * L, (t + 1) * L)
        m = run_ref[0, :, cols]
        top = jnp.max(m, 0, keepdims=True)
        mf_ref[:, cols] = top
        tmp_ref[0, t:t + 1, :] = top
        tmp_ref[1, t:t + 1, :] = jnp.sum(run_ref[1, :, cols] * jnp.exp2(m - top), 0, keepdims=True)

    m_col = tmp_ref[0, 0:NT]
    gx_ref[me_x] = m_col + jnp.log2(tmp_ref[1, 0:NT])
    gX = exchange(lambda peer: gx_ref.at[me_x], gx_ref.at[me_x], me_x, NX, dev_x)

    def settle(first, last):
        def body(i, _):
            rows = ds(i * RC, RC)
            for t in range(T2 // CB):
                lanes = slice(t * CB, (t + 1) * CB)
                fix = jnp.exp2(cm_ref[i, :, lanes] - mf_ref[:, lanes])
                e = (p_ref[rows, lanes].reshape(RC // 8, 8, CB) * fix).reshape(RC, CB)
                p_ref[rows, lanes] = e
                hi = e.astype(BF16)
                hi_ref[rows, lanes] = hi
                lo_ref[rows, lanes] = (e - hi.astype(F32)).astype(BF16)
            return 0

        lax.fori_loop(first, last, body, 0)

    steps = S2 // RC
    settle(0, steps // 2)
    arrived(gX)
    gz_ref[me_z] = lse2(gx_ref, NX)
    gZ = exchange(lambda peer: gz_ref.at[me_z], gz_ref.at[me_z], me_z, NZ, dev_z)
    settle(steps // 2, steps)
    arrived(gZ)
    g_lse = lse2(gz_ref, NZ)
    k = jnp.exp2(m_col - g_lse)
    k_ref[...] = k
    b_mine = lb_ref[ds(me_c * NT, NT), :]
    w_ref[...] = k * jnp.exp(b_mine)

    def row_dots(i, _):
        rows = ds(i * RS, RS)
        acc = jnp.zeros((RS, L), F32)
        for t in range(NT):
            acc += p_ref[rows, t * L:(t + 1) * L] * w_ref[t:t + 1, :]
        sm_ref[rows, :] = acc
        return 0

    lax.fori_loop(0, S2 // RS, row_dots, 0)
    for i in range(NR):
        frc_ref[me_c, i:i + 1, :] = jnp.sum(sm_ref[i * L:(i + 1) * L, :].T, 0, keepdims=True)
    f2c = exchange(lambda peer: frc_ref.at[me_c], frc_ref.at[me_c], me_c, 2, dev_c)
    arrived(f2c)
    fr_ref[me_y] = add_up(frc_ref, 2)
    f2 = exchange(lambda peer: fr_ref.at[me_y], fr_ref.at[me_y], me_y, NY, dev_y)
    arrived(f2)
    total = add_up(fr_ref, NY)
    scale = jnp.exp(la) / total
    a_ref[...] = scale
    spread(scale)

    def column_dots(b, _):
        cols = ds(b * CB, CB)

        def step(i, acc):
            rows = ds(i * RS, RS)
            v = jnp.concatenate([vb_ref[rows, :]] * NX, 1)
            return acc + jnp.sum((p_ref[rows, cols] * v).reshape(RS // 8, 8, CB), 0)

        acc = lax.fori_loop(0, S2 // RS, step, jnp.zeros((8, CB), F32), unroll=2)
        acc = jnp.sum(acc, 0, keepdims=True)
        for t in range(NX):
            tmp_ref[0, pl.ds(b * NX + t, 1), :] = acc[:, t * L:(t + 1) * L]
        return 0

    lax.fori_loop(0, HZ, column_dots, 0)
    cx_ref[me_x] = tmp_ref[0, 0:NT] * k_ref[...]
    cX = exchange(lambda peer: cx_ref.at[me_x], cx_ref.at[me_x], me_x, NX, dev_x)

    mine = lambda v: jnp.where(me_c == 0, v[0:SR], v[SR:NR])
    potential = (jnp.log2(total) - la2 + lse) / BETA
    for i in range(SR):
        x = xs_ref[me_c, :, i * L:(i + 1) * L]
        tmp_ref[1, i:i + 1, :] = jnp.sum(x * x, 0, keepdims=True) / E
    f_ref[...] = tmp_ref[1, 0:SR] - mine(potential)
    write(f_ref, f_out)

    for h in range(2):
        for i in range(SR):
            n = h * SR + i
            parts = split3(xs_ref[h, :, i * L:(i + 1) * L] * scale[n:n + 1, :])
            for j, part in enumerate(parts):
                xa_ref[j * E:(j + 1) * E, n * L:(n + 1) * L] = part

    def pulled(first, last):
        def body(b, _):
            cols = ds(b * CB, CB)
            out = jnp.dot(xa_ref[...], hi_ref[:, cols], preferred_element_type=F32)
            low = jnp.dot(xa_ref[0:2 * E, :], lo_ref[:, cols], preferred_element_type=F32)
            out = out[0:E] + out[E:2 * E] + out[2 * E:3 * E] + low[0:E] + low[E:2 * E]
            for t in range(NX):
                u_ref[t, b] = out[:, t * L:(t + 1) * L] * k_ref[pl.ds(b * NX + t, 1), :]
            return 0

        lax.fori_loop(first, last, body, 0)

    pulled(0, HZ // 2)
    arrived(cX)
    cz_ref[me_z] = add_up(cx_ref, NX)
    cZ = exchange(lambda peer: cz_ref.at[me_z], cz_ref.at[me_z], me_z, NZ, dev_z)
    H2 = HZ // 2
    uX = exchange(lambda peer: u_ref.at[peer, 0:H2], r1_ref.at[me_x, 0:H2], me_x, NX, dev_x)
    pulled(H2, HZ)
    uX += exchange(lambda peer: u_ref.at[peer, H2:HZ], r1_ref.at[me_x, H2:HZ], me_x, NX, dev_x)
    arrived(cZ)
    d = add_up(cz_ref, NZ)
    d_ref[...] = d
    tmp_ref[0, 0:NT] = w_ref[...] / d

    def prep_b(b, _):
        cols = ds(b * CB, CB)
        right = jnp.concatenate([tmp_ref[0, pl.ds(b * NX + t, 1), :] for t in range(NX)], 1)
        for j, part in enumerate(split3(y_ref[:, cols] * right)):
            yb_ref[j * E:(j + 1) * E, cols] = part
        b1, b2, b3 = split3(right)
        row = lax.broadcasted_iota(jnp.int32, (E, CB), 0)
        pick = lambda n, v: jnp.where(row == n, jnp.broadcast_to(v.astype(F32), (E, CB)), 0.0)
        yb_ref[3 * E:4 * E, cols] = (pick(0, b1) + pick(1, b2) + pick(2, b3)).astype(BF16)
        return 0

    lax.fori_loop(0, HZ, prep_b, 0)

    gs_ref[me_c] = (LOG2E * b_mine - g_lse - jnp.log2(d)) / BETA
    gC = exchange(lambda peer: gs_ref.at[me_c], gs_ref.at[me_c], me_c, 2, dev_c)

    core_base = sends.reserve(2)
    tgt_base = sends.reserve(2 * NY)
    RH = RB // 2

    def core_copy(n):
        return sends.copy(so_ref.at[n], sc_ref.at[n], core_base + n, core_base + n, partner)

    def tgt_copy(n, r):
        sem = tgt_base + n * NY + r
        return sends.copy(sy_ref.at[n, r], sr_ref.at[n, me_y], sem, sem, dev_y(lax.rem(me_y + r, NY)))

    owners = [lax.rem(me_y + r, NY) for r in range(NY)]

    def dots(h, n):
        nt = (((1,), (1,)), ((), ()))
        block = lambda ref: jnp.concatenate([ref[ds(h * S + j * RB + n * RH, RH), :] for j in owners], 0)
        out = lax.dot_general(block(hi_ref), yb_ref[...], nt, preferred_element_type=F32)
        return out + lax.dot_general(block(lo_ref), yb_ref[...], nt, preferred_element_type=F32)

    def terms(h, n, out):
        out = out.T
        mass = out[3 * E:3 * E + 1] + out[3 * E + 1:3 * E + 2] + out[3 * E + 2:3 * E + 3]
        out = out[0:E] + out[E:2 * E] + out[2 * E:3 * E]
        result = []
        for r, j in enumerate(owners):
            here = slice(r * RH, (r + 1) * RH)
            x = xs_ref[h, :, ds(j * RB + n * RH, RH)]
            first = h * SR + (j * RB + n * RH) // L
            a = jnp.concatenate([a_ref[pl.ds(first + t, 1), :] for t in range(RH // L)], 1)
            result.append((x * mass[:, here] - out[:, here]) * a)
        return result

    def to_partner(n, out):
        for r, term in enumerate(terms(other, n, out)):
            so_ref[n, owners[r]] = term
        core_copy(n).start()

    def to_owners(n, out):
        core_copy(n).wait_recv()
        for r, term in enumerate(terms(me_c, n, out)):
            term = term + sc_ref[n, owners[r]]
            if r == 0:
                sr_ref[n, me_y] = term
            else:
                sy_ref[n, r] = term
        for r in far_first(NY):
            tgt_copy(n, r).start()

    out0 = dots(other, 0)
    out1 = dots(other, 1)
    to_partner(0, out0)
    to_partner(1, out1)
    out2 = dots(me_c, 0)
    to_owners(0, out2)

    arrived(uX)
    for j in range(HZ):
        total = u_ref[me_x, j]
        for r in range(1, NX):
            total = total + r1_ref[lax.rem(me_x + r, NX), j]
        t2_ref[j] = total
    z_base = sends.reserve(NZ)
    first_z = me_c * HZ
    holds = me_z // HZ == me_c

    def z_copy(j, sender):
        return sends.copy(t2_ref.at[j], r2_ref.at[sender], z_base + j, z_base + sender, dev_z(first_z + j))

    for j in range(HZ):
        @pl.when(first_z + j != me_z)
        def _():
            z_copy(j, me_z).start()

    out3 = dots(me_c, 1)
    to_owners(1, out3)

    sY = []
    for n in range(2):
        for r in range(1, NY):
            tgt_copy(n, r).wait_recv()
        sgb_ref[n, me_y] = add_up(sr_ref.at[n], NY)
        sY.append(exchange(lambda peer: sgb_ref.at[n, me_y], sgb_ref.at[n, me_y], me_y, NY, dev_y))
        write(sgb_ref.at[n, me_y], sg_out.at[:, ds(me_y * RB + n * RH, RH)])

    tile_base = sends.reserve(1)
    tile_copy = sends.copy(tile_ref, tile_ref, tile_base, tile_base, partner)

    @pl.when(holds)
    def _():
        for j in range(NZ):
            @pl.when(j != me_z)
            def _():
                z_copy(0, j).wait_recv()

        total = t2_ref[me_z - first_z]
        for r in range(1, NZ):
            total = total + r2_ref[lax.rem(me_z + r, NZ)]
        here = (me_z - first_z) * NX + me_x
        b = jnp.exp(lb_ref[pl.ds(me_z * NX + me_x, 1), :])
        y = y_ref[:, ds(here * L, L)]
        tile_ref[...] = b * (y - total / d_ref[pl.ds(here, 1), :])
        tile_copy.start()

    @pl.when(jnp.logical_not(holds))
    def _():
        tile_copy.wait_recv()

    tile = tile_ref[...]
    tg_ref[:, 0, :] = jnp.where(me_c == 0, tile[:, 0:E], tile[:, E:2 * E])
    write(tg_ref, tg_out)

    arrived(gC)
    for j in range(2):
        write(gs_ref.at[j], g_out.at[j * NT:(j + 1) * NT])

    for n in range(2):
        for r in range(1, NY):
            sY[n][r - 1].wait_recv()
            j = lax.rem(me_y + NY - r, NY)
            write(sgb_ref.at[n, j], sg_out.at[:, ds(j * RB + n * RH, RH)])

    for copy in writes:
        copy.wait()
    for copy in sends.live:
        copy.wait_send()
    for n in range(2):
        core_copy(n).wait_send()
        for r in range(1, NY):
            tgt_copy(n, r).wait_send()
    for j in range(HZ):
        @pl.when(first_z + j != me_z)
        def _():
            z_copy(j, me_z).wait_send()

    @pl.when(holds)
    def _():
        tile_copy.wait_send()


def finish_kernel(*refs):
    n = len(refs) // 2
    for i in range(n):
        refs[n + i][...] = refs[i][...]


def finish(*arrays):
    return pl.pallas_call(
        finish_kernel,
        out_shape=tuple(jax.ShapeDtypeStruct(a.shape, a.dtype) for a in arrays),
        in_specs=[pl.BlockSpec(memory_space=pltpu.VMEM)] * len(arrays),
        out_specs=[pl.BlockSpec(memory_space=pltpu.VMEM)] * len(arrays),
        compiler_params=pltpu.CompilerParams(vmem_limit_bytes=58 * 1024 * 1024),
        name="results",
    )(*arrays)


def local(dims, x, y, la, lb):
    NX, NZ, NY = dims
    E, S = x.shape
    T = y.shape[1]
    S2, T2 = 2 * S, T // 2
    HZ, RB = NZ // 2, S // NY
    NT, NR, SR = T2 // L, S2 // L, S // L
    n_sems = 2 + 2 * NY + 4 * (NX - 1) + 2 * (NZ - 1) + 1 + 2 + 2 * NY + NZ + 2 * (NY - 1) + 1
    big = max(NT, NR)
    vmem = lambda shape, dtype=F32: pltpu.VMEM(shape, dtype)
    f, g, sg, tg = pl.pallas_call(
        functools.partial(kernel, dims),
        out_shape=(
            jax.ShapeDtypeStruct((SR, L), F32),
            jax.ShapeDtypeStruct((2 * NT, L), F32),
            jax.ShapeDtypeStruct((E, S), F32),
            jax.ShapeDtypeStruct((E, 1, 64), F32),
        ),
        in_specs=[pl.BlockSpec(memory_space=pl.ANY if i < 2 else pltpu.VMEM) for i in range(4)],
        out_specs=[pl.BlockSpec(memory_space=pl.ANY)] * 4,
        scratch_shapes=[
            vmem((S2, T2)), vmem((S2, T2), BF16), vmem((S2, T2), BF16),
            vmem((S2, 8 * E), BF16), vmem((8 * E, T2), BF16),
            vmem((S2, L)), vmem((S2, L)), vmem((S2, L)),
            vmem((S2 // RC, 8, T2)), vmem((1, T2)),
            vmem((2, E, S)), vmem((2, SR, L)), vmem((2, big, L)),
            vmem((2, 8, T2)), vmem((2, NR, L)), vmem((NY, NR, L)), vmem((2, NR, L)), vmem((NY, NR, L)),
            vmem((NX, NT, L)), vmem((NX, NT, L)), vmem((NZ, NT, L)), vmem((NT, L)), vmem((NT, L)),
            vmem((NR, L)), vmem((3 * E, S2), BF16), vmem((4 * E, T2), BF16),
            vmem((NX, NT, L)), vmem((NZ, NT, L)), vmem((NT, L)), vmem((2, NT, L)),
            vmem((NX, HZ, E, L)), vmem((NX, HZ, E, L)), vmem((HZ, E, L)), vmem((NZ, E, L)), vmem((E, L)),
            vmem((2, NY, E, RB // 2)), vmem((2, NY, E, RB // 2)),
            vmem((2, NY, E, RB // 2)), vmem((2, NY, E, RB // 2)), vmem((2, NY, E, RB // 2)),
            vmem((E, T2)), vmem((SR, L)), vmem((E, 1, 64)),
            pltpu.SemaphoreType.DMA((n_sems,)), pltpu.SemaphoreType.DMA((n_sems,)), pltpu.SemaphoreType.DMA((HZ + 1,)),
            pltpu.SemaphoreType.DMA((4 + 2 * NY,)),
        ],
        compiler_params=pltpu.CompilerParams(
            collective_id=0, has_side_effects=True, vmem_limit_bytes=58 * 1024 * 1024
        ),
        cost_estimate=pl.CostEstimate(
            flops=2 * S2 * T2 * (8 + 5 + 8) * E, bytes_accessed=8 * E * (S + T), transcendentals=2 * S2 * T2
        ),
        name="sinkhorn",
    )(x, y, la.reshape(SR, L), lb.reshape(2 * NT, L))
    f, g, sg, tg = finish(f, g, sg, tg)
    return f.reshape(S), g.reshape(T), sg, tg


def solution(mesh):
    n_src, n_tgt = mesh.shape["src"], mesh.shape["tgt"]
    n_x = int(round((n_src // 4) ** 0.5))
    dims = (n_x, n_src // (2 * n_x), n_tgt)
    placed = (P(None, "src"), P(None, "tgt"), P("src"), P("tgt"))
    return jax.shard_map(
        functools.partial(local, dims),
        mesh=mesh,
        in_specs=placed,
        out_specs=(P("src"), P("tgt"), P(None, "src"), P(None, "tgt", "src")),
        check_vma=False,
    )
```

```python
import functools

import jax
import jax.numpy as jnp
import numpy as np
from jax import lax
from jax.experimental import pallas as pl
from jax.experimental.pallas import tpu as pltpu
from jax.sharding import PartitionSpec as P

EPSILON = 0.05
LOG2E = float(np.log2(np.e))
BETA = LOG2E / EPSILON
MESH = pl.DeviceIdType.MESH
F32 = jnp.float32
BF16 = jnp.bfloat16
RS = 128
RC = 64
L = 128


def split3(a):
    hi = a.astype(BF16)
    rest = a - hi.astype(F32)
    mid = rest.astype(BF16)
    lo = (rest - mid.astype(F32)).astype(BF16)
    return hi, mid, lo


def ds(start, size):
    return pl.ds(pl.multiple_of(start, size), size)


def lse2(ref, n):
    top = ref[0]
    for j in range(1, n):
        top = jnp.maximum(top, ref[j])
    total = jnp.exp2(ref[0] - top)
    for j in range(1, n):
        total = total + jnp.exp2(ref[j] - top)
    return top + jnp.log2(total)


def add_up(ref, n):
    total = ref[0]
    for j in range(1, n):
        total = total + ref[j]
    return total


def far_first(n):
    return sorted(range(1, n), key=lambda r: -min(r, n - r))


class Sends:
    def __init__(self, send_sems, recv_sems):
        self.send_sems, self.recv_sems = send_sems, recv_sems
        self.taken = 0
        self.live = []

    def reserve(self, n):
        self.taken += n
        return self.taken - n

    def copy(self, src, dst, send, recv, device):
        return pltpu.make_async_remote_copy(
            src_ref=src,
            dst_ref=dst,
            send_sem=self.send_sems.at[send],
            recv_sem=self.recv_sems.at[recv],
            device_id=device,
            device_id_type=MESH,
        )

    def exchange(self, src, dst, me, n, device):
        base = self.reserve(n - 1)
        copies = []
        for r in range(1, n):
            peer = lax.rem(me + r, n)
            copies.append(self.copy(src(peer), dst, base + r - 1, base + r - 1, device(peer)))
        for r in far_first(n):
            copies[r - 1].start()
        self.live += copies
        return copies


def arrived(copies):
    for copy in copies:
        copy.wait_recv()


def kernel(dims, x_hbm, y_hbm, la_ref, lb_ref,
           f_out, g_out, sg_out, tg_out,
           p_ref, hi_ref, lo_ref, xk_ref, yk_ref, mx_ref, sm_ref, vb_ref, cm_ref, mf_ref,
           xs_ref, las_ref, tmp_ref, run_ref, fc_ref, fm_ref, frc_ref, fr_ref, gm_ref, gx_ref, gz_ref, k_ref, w_ref,
           a_ref, xa_ref, yb_ref, cx_ref, cz_ref, d_ref, gs_ref,
           u_ref, r1_ref, t2_ref, r2_ref, tile_ref, so_ref, sc_ref, sy_ref, sr_ref, sgb_ref,
           y_ref, f_ref, tg_ref, send_sems, recv_sems, y_sems, out_sems):
    NX, NZ, NY = dims
    NQ = 2 * NX
    E, S = x_hbm.shape
    T = y_hbm.shape[1]
    T2, S2 = T // 2, 2 * S
    HZ = NZ // 2
    CB = NX * L
    RB = S // NY
    NT, NR, SR = T2 // L, S2 // L, S // L

    src = lax.axis_index("src")
    me_y = lax.axis_index("tgt")
    me_z = src // NQ
    me_q = lax.rem(src, NQ)
    me_x = me_q // 2
    me_c = lax.rem(me_q, 2)
    other = 1 - me_c
    chip = src - me_c

    dev_c = lambda j: {"src": chip + j}
    dev_y = lambda j: {"tgt": j}
    dev_z = lambda j: {"src": j * NQ + me_q}
    dev_x = lambda j: {"src": me_z * NQ + j * 2 + me_c}
    partner = {"src": chip + other}

    sends = Sends(send_sems, recv_sems)
    exchange = sends.exchange

    loads = [
        pltpu.make_async_copy(
            y_hbm.at[:, ds(me_c * T2 + b * CB, CB)], y_ref.at[:, b * CB:(b + 1) * CB], y_sems.at[b]
        )
        for b in range(HZ)
    ]
    writes = []

    def write(src_ref, out_ref):
        copy = pltpu.make_async_copy(src_ref, out_ref, out_sems.at[len(writes)])
        copy.start()
        writes.append(copy)

    barrier = pltpu.get_barrier_semaphore()
    greeted = 0
    for me, n, device in ((me_z, NZ, dev_z), (me_x, NX, dev_x), (me_y, NY, dev_y), (me_c, 2, dev_c)):
        for r in far_first(n):
            pl.semaphore_signal(barrier, inc=1, device_id=device(lax.rem(me + r, n)), device_id_type=MESH)
            greeted += 1

    load_x = pltpu.make_async_copy(x_hbm, xs_ref.at[me_c], y_sems.at[HZ])
    load_x.start()
    for load in loads:
        load.start()

    def prep_y(b, _):
        cols = ds(b * CB, CB)
        y = y_ref[:, cols]
        y1, y2, y3 = split3(y)
        for n, part in enumerate((y1, y2, y1, y3, y2, y1)):
            yk_ref[n * E:(n + 1) * E, cols] = part
        lb = jnp.concatenate([lb_ref[pl.ds(me_c * NT + b * NX + t, 1), :] for t in range(NX)], 1)
        u = LOG2E * lb - (BETA / E) * jnp.sum(y * y, 0, keepdims=True)
        u1, u2, u3 = split3(u)
        row = lax.broadcasted_iota(jnp.int32, (16, CB), 0)
        pick = lambda n, v: jnp.where(row == n, jnp.broadcast_to(v.astype(F32), (16, CB)), 0.0)
        yk_ref[6 * E:6 * E + 16, cols] = (pick(0, u1) + pick(1, u2) + pick(2, u3)).astype(BF16)
        yk_ref[6 * E + 16:8 * E, cols] = jnp.zeros((2 * E - 16, CB), BF16)
        return 0


    lane = lax.broadcasted_iota(jnp.int32, (L, L), 1)
    left = lane < E

    def prep_x(h):
        def body(i, _):
            rows = ds(h * S + i * L, L)
            x = xs_ref[h, :, ds(i * L, L)] * (2.0 * BETA / E)
            x1, x2, x3 = (v.astype(F32) for v in split3(jnp.concatenate([x, x], 0).T))
            xk_ref[rows, 0:128] = x1.astype(BF16)
            xk_ref[rows, 128:256] = jnp.where(left, x2, x1).astype(BF16)
            xk_ref[rows, 256:384] = jnp.where(left, x2, x3).astype(BF16)
            xk_ref[rows, 384:512] = jnp.where(lane < 3, 1.0, 0.0).astype(BF16)
            mx_ref[rows, :] = jnp.full((L, L), -3e38, F32)
            sm_ref[rows, :] = jnp.zeros((L, L), F32)
            return 0

        lax.fori_loop(0, SR, body, 0)

    W2 = T2 // 2

    def scores(h, b):
        yk = yk_ref[:, b * W2:(b + 1) * W2]
        for i in range(S // RS):
            rows = ds(h * S + i * RS, RS)
            s = jnp.dot(xk_ref[rows, :], yk, preferred_element_type=F32)
            p_ref[rows, b * W2:(b + 1) * W2] = s
            old = mx_ref[rows, :]
            m = old
            for t in range(W2 // L):
                m = jnp.maximum(m, s[:, t * L:(t + 1) * L])
            acc = sm_ref[rows, :] * jnp.exp2(old - m)
            for t in range(W2 // L):
                acc = acc + jnp.exp2(s[:, t * L:(t + 1) * L] - m)
            mx_ref[rows, :] = m
            sm_ref[rows, :] = acc

    def merge(h):
        for i in range(SR):
            rows = ds(h * S + i * L, L)
            m = mx_ref[rows, :].T
            top = jnp.max(m, 0, keepdims=True)
            tmp_ref[0, pl.ds(h * SR + i, 1), :] = top
            tmp_ref[1, pl.ds(h * SR + i, 1), :] = jnp.sum(sm_ref[rows, :].T * jnp.exp2(m - top), 0, keepdims=True)

    load_x.wait()
    las_ref[me_c] = la_ref[...]
    prep_x(me_c)
    for load in loads:
        load.wait()
    lax.fori_loop(0, HZ, prep_y, 0)
    scores(me_c, 0)
    pl.semaphore_wait(barrier, greeted)
    base = sends.reserve(2)
    swap = [
        sends.copy(xs_ref.at[me_c], xs_ref.at[me_c], base, base, partner),
        sends.copy(la_ref, las_ref.at[me_c], base + 1, base + 1, partner),
    ]
    for copy in swap:
        copy.start()
    sends.live += swap
    scores(me_c, 1)
    arrived(swap)
    prep_x(other)
    merge(me_c)
    scores(other, 0)
    scores(other, 1)

    merge(other)
    fc_ref[me_c] = tmp_ref[0] + jnp.log2(tmp_ref[1])
    f1c = exchange(lambda peer: fc_ref.at[me_c], fc_ref.at[me_c], me_c, 2, dev_c)

    la = jnp.concatenate([las_ref[0], las_ref[1]], 0)
    la2 = LOG2E * la

    def spread(a):
        for i in range(NR):
            vb_ref[i * L:(i + 1) * L, :] = jnp.broadcast_to(a[i:i + 1, :], (L, L)).T

    arrived(f1c)
    fm_ref[me_y] = lse2(fc_ref, 2)
    f1 = exchange(lambda peer: fm_ref.at[me_y], fm_ref.at[me_y], me_y, NY, dev_y)
    run_ref[0] = jnp.full((8, T2), -3e38, F32)
    run_ref[1] = jnp.zeros((8, T2), F32)
    arrived(f1)
    lse = lse2(fm_ref, NY)
    spread(la2 - lse)

    def columns(i, _):
        rows = ds(i * RC, RC)
        v = jnp.concatenate([vb_ref[rows, :]] * NX, 1)
        for b in range(HZ):
            cols = slice(b * CB, (b + 1) * CB)
            t = (p_ref[rows, cols] + v).reshape(RC // 8, 8, CB)
            old = run_ref[0, :, cols]
            m = jnp.maximum(old, jnp.max(t, 0))
            e = jnp.exp2(t - m)
            p_ref[rows, cols] = e.reshape(RC, CB)
            cm_ref[i, :, cols] = m
            run_ref[0, :, cols] = m
            run_ref[1, :, cols] = run_ref[1, :, cols] * jnp.exp2(old - m) + jnp.sum(e, 0)
        return 0

    lax.fori_loop(0, S2 // RC, columns, 0)
    for t in range(NT):
        cols = slice(t * L, (t + 1) * L)
        m = run_ref[0, :, cols]
        top = jnp.max(m, 0, keepdims=True)
        mf_ref[:, cols] = top
        tmp_ref[0, t:t + 1, :] = top
        tmp_ref[1, t:t + 1, :] = jnp.sum(run_ref[1, :, cols] * jnp.exp2(m - top), 0, keepdims=True)

    m_col = tmp_ref[0, 0:NT]
    gx_ref[me_x] = m_col + jnp.log2(tmp_ref[1, 0:NT])
    gX = exchange(lambda peer: gx_ref.at[me_x], gx_ref.at[me_x], me_x, NX, dev_x)

    def settle(first, last):
        def body(i, _):
            rows = ds(i * RC, RC)
            for t in range(T2 // CB):
                lanes = slice(t * CB, (t + 1) * CB)
                fix = jnp.exp2(cm_ref[i, :, lanes] - mf_ref[:, lanes])
                e = (p_ref[rows, lanes].reshape(RC // 8, 8, CB) * fix).reshape(RC, CB)
                p_ref[rows, lanes] = e
                hi = e.astype(BF16)
                hi_ref[rows, lanes] = hi
                lo_ref[rows, lanes] = (e - hi.astype(F32)).astype(BF16)
            return 0

        lax.fori_loop(first, last, body, 0)

    steps = S2 // RC
    settle(0, steps // 2)
    arrived(gX)
    gz_ref[me_z] = lse2(gx_ref, NX)
    gZ = exchange(lambda peer: gz_ref.at[me_z], gz_ref.at[me_z], me_z, NZ, dev_z)
    settle(steps // 2, steps)
    arrived(gZ)
    g_lse = lse2(gz_ref, NZ)
    k = jnp.exp2(m_col - g_lse)
    k_ref[...] = k
    b_mine = lb_ref[ds(me_c * NT, NT), :]
    w_ref[...] = k * jnp.exp(b_mine)

    def row_dots(i, _):
        rows = ds(i * RS, RS)
        acc = jnp.zeros((RS, L), F32)
        for t in range(NT):
            acc += p_ref[rows, t * L:(t + 1) * L] * w_ref[t:t + 1, :]
        sm_ref[rows, :] = acc
        return 0

    lax.fori_loop(0, S2 // RS, row_dots, 0)
    for i in range(NR):
        frc_ref[me_c, i:i + 1, :] = jnp.sum(sm_ref[i * L:(i + 1) * L, :].T, 0, keepdims=True)
    f2c = exchange(lambda peer: frc_ref.at[me_c], frc_ref.at[me_c], me_c, 2, dev_c)
    arrived(f2c)
    fr_ref[me_y] = add_up(frc_ref, 2)
    f2 = exchange(lambda peer: fr_ref.at[me_y], fr_ref.at[me_y], me_y, NY, dev_y)
    arrived(f2)
    total = add_up(fr_ref, NY)
    scale = jnp.exp(la) / total
    a_ref[...] = scale
    spread(scale)

    def column_dots(b, _):
        cols = ds(b * CB, CB)

        def step(i, acc):
            rows = ds(i * RS, RS)
            v = jnp.concatenate([vb_ref[rows, :]] * NX, 1)
            return acc + jnp.sum((p_ref[rows, cols] * v).reshape(RS // 8, 8, CB), 0)

        acc = lax.fori_loop(0, S2 // RS, step, jnp.zeros((8, CB), F32), unroll=2)
        acc = jnp.sum(acc, 0, keepdims=True)
        for t in range(NX):
            tmp_ref[0, pl.ds(b * NX + t, 1), :] = acc[:, t * L:(t + 1) * L]
        return 0

    lax.fori_loop(0, HZ, column_dots, 0)
    cx_ref[me_x] = tmp_ref[0, 0:NT] * k_ref[...]
    cX = exchange(lambda peer: cx_ref.at[me_x], cx_ref.at[me_x], me_x, NX, dev_x)

    mine = lambda v: jnp.where(me_c == 0, v[0:SR], v[SR:NR])
    potential = (jnp.log2(total) - la2 + lse) / BETA
    for i in range(SR):
        x = xs_ref[me_c, :, i * L:(i + 1) * L]
        tmp_ref[1, i:i + 1, :] = jnp.sum(x * x, 0, keepdims=True) / E
    f_ref[...] = tmp_ref[1, 0:SR] - mine(potential)
    write(f_ref, f_out)

    for h in range(2):
        for i in range(SR):
            n = h * SR + i
            parts = split3(xs_ref[h, :, i * L:(i + 1) * L] * scale[n:n + 1, :])
            for j, part in enumerate(parts):
                xa_ref[j * E:(j + 1) * E, n * L:(n + 1) * L] = part

    def pulled(first, last):
        def body(b, _):
            cols = ds(b * CB, CB)
            out = jnp.dot(xa_ref[...], hi_ref[:, cols], preferred_element_type=F32)
            low = jnp.dot(xa_ref[0:2 * E, :], lo_ref[:, cols], preferred_element_type=F32)
            out = out[0:E] + out[E:2 * E] + out[2 * E:3 * E] + low[0:E] + low[E:2 * E]
            for t in range(NX):
                u_ref[t, b] = out[:, t * L:(t + 1) * L] * k_ref[pl.ds(b * NX + t, 1), :]
            return 0

        lax.fori_loop(first, last, body, 0)

    pulled(0, HZ // 2)
    arrived(cX)
    cz_ref[me_z] = add_up(cx_ref, NX)
    cZ = exchange(lambda peer: cz_ref.at[me_z], cz_ref.at[me_z], me_z, NZ, dev_z)
    H2 = HZ // 2
    uX = exchange(lambda peer: u_ref.at[peer, 0:H2], r1_ref.at[me_x, 0:H2], me_x, NX, dev_x)
    pulled(H2, HZ)
    uX += exchange(lambda peer: u_ref.at[peer, H2:HZ], r1_ref.at[me_x, H2:HZ], me_x, NX, dev_x)
    arrived(cZ)
    d = add_up(cz_ref, NZ)
    d_ref[...] = d
    tmp_ref[0, 0:NT] = w_ref[...] / d

    def prep_b(b, _):
        cols = ds(b * CB, CB)
        right = jnp.concatenate([tmp_ref[0, pl.ds(b * NX + t, 1), :] for t in range(NX)], 1)
        for j, part in enumerate(split3(y_ref[:, cols] * right)):
            yb_ref[j * E:(j + 1) * E, cols] = part
        b1, b2, b3 = split3(right)
        row = lax.broadcasted_iota(jnp.int32, (E, CB), 0)
        pick = lambda n, v: jnp.where(row == n, jnp.broadcast_to(v.astype(F32), (E, CB)), 0.0)
        yb_ref[3 * E:4 * E, cols] = (pick(0, b1) + pick(1, b2) + pick(2, b3)).astype(BF16)
        return 0

    lax.fori_loop(0, HZ, prep_b, 0)

    core_base = sends.reserve(2)
    tgt_base = sends.reserve(2 * NY)
    RH = RB // 2

    def core_copy(n):
        return sends.copy(so_ref.at[n], sc_ref.at[n], core_base + n, core_base + n, partner)

    def tgt_copy(n, r):
        sem = tgt_base + n * NY + r
        return sends.copy(sy_ref.at[n, r], sr_ref.at[n, me_y], sem, sem, dev_y(lax.rem(me_y + r, NY)))

    owners = [lax.rem(me_y + r, NY) for r in range(NY)]

    def dots(h, n):
        nt = (((1,), (1,)), ((), ()))
        block = lambda ref: jnp.concatenate([ref[ds(h * S + j * RB + n * RH, RH), :] for j in owners], 0)
        out = lax.dot_general(block(hi_ref), yb_ref[...], nt, preferred_element_type=F32)
        return out + lax.dot_general(block(lo_ref), yb_ref[...], nt, preferred_element_type=F32)

    def terms(h, n, out):
        out = out.T
        mass = out[3 * E:3 * E + 1] + out[3 * E + 1:3 * E + 2] + out[3 * E + 2:3 * E + 3]
        out = out[0:E] + out[E:2 * E] + out[2 * E:3 * E]
        result = []
        for r, j in enumerate(owners):
            here = slice(r * RH, (r + 1) * RH)
            x = xs_ref[h, :, ds(j * RB + n * RH, RH)]
            first = h * SR + (j * RB + n * RH) // L
            a = jnp.concatenate([a_ref[pl.ds(first + t, 1), :] for t in range(RH // L)], 1)
            result.append((x * mass[:, here] - out[:, here]) * a)
        return result

    def to_partner(n, out):
        for r, term in enumerate(terms(other, n, out)):
            so_ref[n, owners[r]] = term
        core_copy(n).start()

    def to_owners(n, out):
        core_copy(n).wait_recv()
        for r, term in enumerate(terms(me_c, n, out)):
            term = term + sc_ref[n, owners[r]]
            if r == 0:
                sr_ref[n, me_y] = term
            else:
                sy_ref[n, r] = term
        for r in far_first(NY):
            tgt_copy(n, r).start()

    out0 = dots(other, 0)
    out1 = dots(other, 1)
    to_partner(0, out0)
    to_partner(1, out1)
    out2 = dots(me_c, 0)
    to_owners(0, out2)

    arrived(uX)
    for j in range(HZ):
        total = u_ref[me_x, j]
        for r in range(1, NX):
            total = total + r1_ref[lax.rem(me_x + r, NX), j]
        t2_ref[j] = total
    z_base = sends.reserve(NZ)
    first_z = me_c * HZ
    holds = me_z // HZ == me_c

    def z_copy(j, sender):
        return sends.copy(t2_ref.at[j], r2_ref.at[sender], z_base + j, z_base + sender, dev_z(first_z + j))

    for j in range(HZ):
        @pl.when(first_z + j != me_z)
        def _():
            z_copy(j, me_z).start()

    out3 = dots(me_c, 1)
    to_owners(1, out3)

    gs_ref[me_c] = (LOG2E * b_mine - g_lse - jnp.log2(d)) / BETA
    gC = exchange(lambda peer: gs_ref.at[me_c], gs_ref.at[me_c], me_c, 2, dev_c)


    sY = []
    for n in range(2):
        for r in range(1, NY):
            tgt_copy(n, r).wait_recv()
        sgb_ref[n, me_y] = add_up(sr_ref.at[n], NY)
        sY.append(exchange(lambda peer: sgb_ref.at[n, me_y], sgb_ref.at[n, me_y], me_y, NY, dev_y))
        write(sgb_ref.at[n, me_y], sg_out.at[:, ds(me_y * RB + n * RH, RH)])

    tile_base = sends.reserve(1)
    tile_copy = sends.copy(tile_ref, tile_ref, tile_base, tile_base, partner)

    @pl.when(holds)
    def _():
        for j in range(NZ):
            @pl.when(j != me_z)
            def _():
                z_copy(0, j).wait_recv()

        total = t2_ref[me_z - first_z]
        for r in range(1, NZ):
            total = total + r2_ref[lax.rem(me_z + r, NZ)]
        here = (me_z - first_z) * NX + me_x
        b = jnp.exp(lb_ref[pl.ds(me_z * NX + me_x, 1), :])
        y = y_ref[:, ds(here * L, L)]
        tile_ref[...] = b * (y - total / d_ref[pl.ds(here, 1), :])
        tile_copy.start()

    @pl.when(jnp.logical_not(holds))
    def _():
        tile_copy.wait_recv()

    tile = tile_ref[...]
    tg_ref[:, 0, :] = jnp.where(me_c == 0, tile[:, 0:E], tile[:, E:2 * E])
    write(tg_ref, tg_out)

    arrived(gC)
    for j in range(2):
        write(gs_ref.at[j], g_out.at[j * NT:(j + 1) * NT])

    for n in range(2):
        for r in range(1, NY):
            sY[n][r - 1].wait_recv()
            j = lax.rem(me_y + NY - r, NY)
            write(sgb_ref.at[n, j], sg_out.at[:, ds(j * RB + n * RH, RH)])

    for copy in writes:
        copy.wait()
    for copy in sends.live:
        copy.wait_send()
    for n in range(2):
        core_copy(n).wait_send()
        for r in range(1, NY):
            tgt_copy(n, r).wait_send()
    for j in range(HZ):
        @pl.when(first_z + j != me_z)
        def _():
            z_copy(j, me_z).wait_send()

    @pl.when(holds)
    def _():
        tile_copy.wait_send()


def finish_kernel(*refs):
    n = len(refs) // 2
    for i in range(n):
        refs[n + i][...] = refs[i][...]


def finish(*arrays):
    return pl.pallas_call(
        finish_kernel,
        out_shape=tuple(jax.ShapeDtypeStruct(a.shape, a.dtype) for a in arrays),
        in_specs=[pl.BlockSpec(memory_space=pltpu.VMEM)] * len(arrays),
        out_specs=[pl.BlockSpec(memory_space=pltpu.VMEM)] * len(arrays),
        compiler_params=pltpu.CompilerParams(vmem_limit_bytes=58 * 1024 * 1024),
        name="results",
    )(*arrays)


def local(dims, x, y, la, lb):
    NX, NZ, NY = dims
    E, S = x.shape
    T = y.shape[1]
    S2, T2 = 2 * S, T // 2
    HZ, RB = NZ // 2, S // NY
    NT, NR, SR = T2 // L, S2 // L, S // L
    n_sems = 2 + 2 * NY + 4 * (NX - 1) + 2 * (NZ - 1) + 1 + 2 + 2 * NY + NZ + 2 * (NY - 1) + 1
    big = max(NT, NR)
    vmem = lambda shape, dtype=F32: pltpu.VMEM(shape, dtype)
    f, g, sg, tg = pl.pallas_call(
        functools.partial(kernel, dims),
        out_shape=(
            jax.ShapeDtypeStruct((SR, L), F32),
            jax.ShapeDtypeStruct((2 * NT, L), F32),
            jax.ShapeDtypeStruct((E, S), F32),
            jax.ShapeDtypeStruct((E, 1, 64), F32),
        ),
        in_specs=[pl.BlockSpec(memory_space=pl.ANY if i < 2 else pltpu.VMEM) for i in range(4)],
        out_specs=[pl.BlockSpec(memory_space=pl.ANY)] * 4,
        scratch_shapes=[
            vmem((S2, T2)), vmem((S2, T2), BF16), vmem((S2, T2), BF16),
            vmem((S2, 8 * E), BF16), vmem((8 * E, T2), BF16),
            vmem((S2, L)), vmem((S2, L)), vmem((S2, L)),
            vmem((S2 // RC, 8, T2)), vmem((1, T2)),
            vmem((2, E, S)), vmem((2, SR, L)), vmem((2, big, L)),
            vmem((2, 8, T2)), vmem((2, NR, L)), vmem((NY, NR, L)), vmem((2, NR, L)), vmem((NY, NR, L)),
            vmem((NX, NT, L)), vmem((NX, NT, L)), vmem((NZ, NT, L)), vmem((NT, L)), vmem((NT, L)),
            vmem((NR, L)), vmem((3 * E, S2), BF16), vmem((4 * E, T2), BF16),
            vmem((NX, NT, L)), vmem((NZ, NT, L)), vmem((NT, L)), vmem((2, NT, L)),
            vmem((NX, HZ, E, L)), vmem((NX, HZ, E, L)), vmem((HZ, E, L)), vmem((NZ, E, L)), vmem((E, L)),
            vmem((2, NY, E, RB // 2)), vmem((2, NY, E, RB // 2)),
            vmem((2, NY, E, RB // 2)), vmem((2, NY, E, RB // 2)), vmem((2, NY, E, RB // 2)),
            vmem((E, T2)), vmem((SR, L)), vmem((E, 1, 64)),
            pltpu.SemaphoreType.DMA((n_sems,)), pltpu.SemaphoreType.DMA((n_sems,)), pltpu.SemaphoreType.DMA((HZ + 1,)),
            pltpu.SemaphoreType.DMA((4 + 2 * NY,)),
        ],
        compiler_params=pltpu.CompilerParams(
            collective_id=0, has_side_effects=True, vmem_limit_bytes=58 * 1024 * 1024
        ),
        cost_estimate=pl.CostEstimate(
            flops=2 * S2 * T2 * (8 + 5 + 8) * E, bytes_accessed=8 * E * (S + T), transcendentals=2 * S2 * T2
        ),
        name="sinkhorn",
    )(x, y, la.reshape(SR, L), lb.reshape(2 * NT, L))
    f, g, sg, tg = finish(f, g, sg, tg)
    return f.reshape(S), g.reshape(T), sg, tg


def solution(mesh):
    n_src, n_tgt = mesh.shape["src"], mesh.shape["tgt"]
    n_x = int(round((n_src // 4) ** 0.5))
    dims = (n_x, n_src // (2 * n_x), n_tgt)
    placed = (P(None, "src"), P(None, "tgt"), P("src"), P("tgt"))
    return jax.shard_map(
        functools.partial(local, dims),
        mesh=mesh,
        in_specs=placed,
        out_specs=(P("src"), P("tgt"), P(None, "src"), P(None, "tgt", "src")),
        check_vma=False,
    )
```
